512 devices in a mesh: dom: 32 (over x, z_hi, core), band: 16 (over z_lo, y).
Axes of the slice: x: 4, y: 8, z: 8 (z_hi: 4, z_lo: 2; z = z_hi * 2 + z_lo), core: 2. Of those that a mesh axis runs over, the one named last changes fastest.
Arguments:
- wave_block: float32 [16, 384, 16, 128], P('band', 'dom'), may hold values from -6 to 6
- potential: float32 [384, 16, 128], P('dom'), may hold values from -1.5 to 1
- projectors: float32 [1024, 8, 2048], P('dom', None, 'band'), may hold values from -0.25 to 0.25
- kb_energy: float32 [512, 8], P('dom'), may hold values from 1 to 6
- slot_atom: int32 [1024], P('dom'), may hold values from 0 to 511, as said below
- slot_corner: int32 [3, 1024], P(None, 'dom'), may hold values from 0 to 112, as said below
Outputs:
- filtered: float32 [16, 384, 16, 128], P('band', 'dom')
The draws below stay inside these ranges and needn't reach their ends.
Inputs may be any that keep to these rules, and one draw needn't show every extreme that they name: `slot_atom`: the slots of slab t are rows t * 32 to (t + 1) * 32 - 1; each names an atom owned by slab t - 1, t or t + 1, where atom a is owned by slab a // 16. `slot_corner`: rows 0, 1, 2 give the box's first cell inside its slab along the three dimensions, at most 4, 0 and 112.
All inputs are finite; a program needn't handle non-finite values.
Results may differ from the reference program's by a relative error of at most 0.00024.
Values sent between devices are 32-bit elements; how exact they have to be, the bound alone decides.
A program may use at most 64 MiB of HBM per device.

```python
import jax
import jax.numpy as jnp
from jax import lax

PROJ = 8
SX = 8
SY = 16
SZ = 16
DEGREE = 3
CX = 12
CY = 16
CZ = 128
ATOM_DEV = 16
SLOTS = 32
SUP = 2048
NX = 384
BANDS = 16
ATOMS = 512
TOTAL_SLOTS = 1024


def draw_slot_atom(key, part):
    key_side, key_pick = jax.random.split(key)
    slot_ids = jnp.arange(TOTAL_SLOTS, dtype=jnp.int32)
    tile_ids = slot_ids // SLOTS
    within = slot_ids % SLOTS
    tile_count = TOTAL_SLOTS // SLOTS
    side_step = jax.random.randint(key_side, (TOTAL_SLOTS,), -1, 2)
    owner_tile = jnp.clip(tile_ids + side_step, 0, tile_count - 1)
    picked = jax.random.randint(key_pick, (TOTAL_SLOTS,), 0, ATOM_DEV)
    atom_ids = owner_tile * ATOM_DEV + picked
    atom_ids = jnp.where(within == 0, tile_ids * ATOM_DEV + ATOM_DEV - 1, atom_ids)
    atom_ids = jnp.where(within == 1, tile_ids * ATOM_DEV, atom_ids)
    return atom_ids.astype(jnp.int32)


def draw_slot_corner(key, part):
    key_list = jax.random.split(key, 3)
    within = jnp.arange(TOTAL_SLOTS, dtype=jnp.int32) % SLOTS
    corner_rows = []
    for axis_pos, limits in enumerate(((CX, SX), (CY, SY), (CZ, SZ))):
        top_corner = limits[0] - limits[1]
        drawn = jax.random.randint(key_list[axis_pos], (TOTAL_SLOTS,), 0, top_corner + 1)
        drawn = jnp.where(within == 0, 0, drawn)
        drawn = jnp.where(within == 1, top_corner, drawn)
        corner_rows.append(drawn)
    return jnp.stack(corner_rows).astype(jnp.int32)


def levels(rng, shape, cuts, smallest, high):
    def one(axis_at, shards_of):
        steps = jax.random.uniform(jax.random.fold_in(jax.random.fold_in(rng, 6), axis_at), (shards_of,), jnp.float32, smallest / len(cuts), high / len(cuts))
        return jnp.repeat(jnp.exp(steps), shape[axis_at] // shards_of).reshape((-1,) + (1,) * (len(shape) - axis_at - 1))

    gain = one(*cuts[0])
    for cut in cuts[1:]:
        gain = gain * one(*cut)
    return gain


def scatter_about(key, extent, scale, reach, cuts=(), kind=jnp.bfloat16):
    factor_of = levels(key, extent, cuts, -0.22, 0.18) if cuts else 1.0
    entries = jax.random.normal(key, extent, jnp.float32) * scale * factor_of
    return jnp.minimum(jnp.maximum(entries, -reach), reach).astype(kind)


def setup_inputs(seed: int = 0) -> dict:
    key_of = jax.random.split(jax.random.key(seed), 7)
    wave_block = scatter_about(key_of[0], (BANDS, NX, CY, CZ), 1.0, 6.0, ((0, 16), (1, 32)), jnp.float32)
    potential = jnp.clip(-1.5 + 2.5 * jax.random.uniform(key_of[1], (NX, CY, CZ), jnp.float32) ** levels(key_of[1], (NX, CY, CZ), ((0, 32),), -0.2, 0.2), -1.5, 1.0)
    projectors = scatter_about(key_of[2], (TOTAL_SLOTS, PROJ, SUP), (SUP // 4) ** -0.5, 0.25, ((0, 32), (2, 16)), jnp.float32)
    kb_energy = jnp.clip(1.0 + 5.0 * jax.random.uniform(key_of[3], (ATOMS, PROJ), jnp.float32) ** levels(key_of[3], (ATOMS, PROJ), ((0, 32),), -0.2, 0.2), 1.0, 6.0)
    slot_atom = draw_slot_atom(jax.random.fold_in(key_of[6], 71), 0)
    slot_corner = draw_slot_corner(jax.random.fold_in(key_of[6], 71), 0)
    return {"wave_block": wave_block, "potential": potential, "projectors": projectors, "kb_energy": kb_energy, "slot_atom": slot_atom, "slot_corner": slot_corner}


STENCIL_WEIGHTS = (-5369.0 / 1800.0, 12.0 / 7.0, -15.0 / 56.0, 10.0 / 189.0, -1.0 / 112.0, 2.0 / 1925.0, -1.0 / 16632.0)
LOWER_EDGE = 3.0
UPPER_EDGE = 30.0
ANCHOR_POINT = 0.5
EXACT = lax.Precision.HIGHEST


def laplacian(padded, reach_cells):
    extent_list = [padded.shape[axis_pos] - 2 * reach_cells for axis_pos in (-3, -2, -1)]

    def window(shift_x, shift_y, shift_z):
        return padded[..., reach_cells + shift_x:reach_cells + shift_x + extent_list[0],
                      reach_cells + shift_y:reach_cells + shift_y + extent_list[1],
                      reach_cells + shift_z:reach_cells + shift_z + extent_list[2]]

    summed = 3.0 * STENCIL_WEIGHTS[0] * window(0, 0, 0)
    for offset in range(1, reach_cells + 1):
        neighbours = window(offset, 0, 0) + window(-offset, 0, 0)
        neighbours = neighbours + window(0, offset, 0) + window(0, -offset, 0)
        neighbours = neighbours + window(0, 0, offset) + window(0, 0, -offset)
        summed = summed + STENCIL_WEIGHTS[offset] * neighbours
    return summed


def extract_boxes(field_block, corners):
    band_count = field_block.shape[0]

    def one_box(corner_x, corner_y, corner_z):
        zero_index = jnp.zeros((), jnp.int32)
        box_cut = lax.dynamic_slice(field_block, (zero_index, corner_x, corner_y, corner_z), (band_count, SX, SY, SZ))
        return box_cut.reshape(band_count, SX * SY * SZ)

    return jax.vmap(one_box)(corners[0], corners[1], corners[2])


def deposit_boxes(base_field, values, corners):
    band_count = base_field.shape[0]
    piece_shape = (band_count, SX, SY, SZ)

    def add_one(slot_pos, accumulated):
        zero_index = jnp.zeros((), jnp.int32)
        start_list = (zero_index, corners[0, slot_pos], corners[1, slot_pos], corners[2, slot_pos])
        current = lax.dynamic_slice(accumulated, start_list, piece_shape)
        return lax.dynamic_update_slice(accumulated, current + values[slot_pos].reshape(piece_shape), start_list)

    return lax.fori_loop(0, values.shape[0], add_one, base_field)


def chebyshev_filter(start_block, apply_fn):
    half_width = (UPPER_EDGE - LOWER_EDGE) / 2.0
    centre = (UPPER_EDGE + LOWER_EDGE) / 2.0
    sigma_first = half_width / (ANCHOR_POINT - centre)
    previous = start_block
    current = (sigma_first / half_width) * (apply_fn(start_block) - centre * start_block)
    sigma_now = sigma_first
    for degree in range(2, DEGREE + 1):
        sigma_next = 1.0 / (2.0 / sigma_first - sigma_now)
        following = (2.0 * sigma_next / half_width) * (apply_fn(current) - centre * current) - (sigma_now * sigma_next) * previous
        previous, current, sigma_now = current, following, sigma_next
    return current


def reference(wave_block, potential, projectors, kb_energy, slot_atom, slot_corner):
    slot_total = slot_atom.shape[0]
    tile_of_slot = jnp.arange(slot_total, dtype=jnp.int32) // SLOTS
    corners = jnp.stack([slot_corner[0] + tile_of_slot * CX, slot_corner[1], slot_corner[2]]).astype(jnp.int32)
    atom_total = kb_energy.shape[0]
    reach_cells = len(STENCIL_WEIGHTS) - 1

    def apply_h(field_block):
        padded = jnp.pad(field_block, ((0, 0), (reach_cells, reach_cells), (reach_cells, reach_cells), (reach_cells, reach_cells)))
        kinetic = -0.5 * laplacian(padded, reach_cells)
        box_values = extract_boxes(field_block, corners)
        projected = jnp.einsum('spc,sbc->spb', projectors, box_values, precision=EXACT)
        atom_sums = jax.ops.segment_sum(projected, slot_atom, num_segments=atom_total)
        scaled = atom_sums * kb_energy[:, :, None]
        returned = scaled[slot_atom]
        values = jnp.einsum('spc,spb->sbc', projectors, returned, precision=EXACT)
        return deposit_boxes(kinetic + potential[None] * field_block, values, corners)

    def one_band(band_field):
        return chebyshev_filter(band_field[None], apply_h)[0]

    return lax.map(one_band, wave_block)
```

```python
import jax
import jax.numpy as jnp
from jax import lax
from jax.experimental import pallas as pl
from jax.experimental.pallas import tpu as pltpu
from jax.sharding import PartitionSpec as P

SX, SY, SZ, DEGREE, PROJ = 8, 16, 16, 3, 8
CX, CY, CZ = 12, 16, 128
SLOTS, ATOM_DEV = 32, 16
LANES = SLOTS * SZ
ROWS = CX * CY
REACH = 6
Y_RING = 8
PARTS = 4
HALF = PARTS // 2
PROJ_PART = PROJ // PARTS
SENDS = 5 * PARTS
STENCIL = (
    -5369.0 / 1800.0,
    12.0 / 7.0,
    -15.0 / 56.0,
    10.0 / 189.0,
    -1.0 / 112.0,
    2.0 / 1925.0,
    -1.0 / 16632.0,
)
KINETIC = tuple(-0.5 * weight for weight in STENCIL)
LOWER_EDGE, UPPER_EDGE, ANCHOR_POINT = 3.0, 30.0, 0.5
F32, BF16 = jnp.float32, jnp.bfloat16
MESH = pl.DeviceIdType.MESH
REACHED = (1, 2, -1, -2)


def split(x):
    high = x.astype(BF16)
    return high, (x - high.astype(F32)).astype(BF16)


def dot(a, b):
    return jnp.dot(a, b, preferred_element_type=F32)


def iota(shape, dim):
    return lax.broadcasted_iota(jnp.int32, shape, dim)


def weight_at(distance, centre):
    out = jnp.where(distance == 0, F32(centre), F32(0.0))
    for k in range(1, REACH + 1):
        out = jnp.where(distance == k, F32(KINETIC[k]), out)
    return out


def coefficients():
    half_width = (UPPER_EDGE - LOWER_EDGE) / 2.0
    centre = (UPPER_EDGE + LOWER_EDGE) / 2.0
    sigma_first = half_width / (ANCHOR_POINT - centre)
    out = [(sigma_first / half_width, 0.0)]
    sigma = sigma_first
    for _ in range(2, DEGREE + 1):
        following = 1.0 / (2.0 / sigma_first - sigma)
        out.append((2.0 * following / half_width, sigma * following))
        sigma = following
    return centre, out


def transposed_parts(x):
    row, col = iota((8, 128), 0), iota((8, 128), 1) >> 4
    for bit in (1, 2, 4):
        row_bit, col_bit = (row & bit) != 0, (col & bit) != 0
        down = pltpu.roll(pltpu.roll(x, bit, 0), 128 - 16 * bit, 1)
        up = pltpu.roll(pltpu.roll(x, 8 - bit, 0), 16 * bit, 1)
        x = jnp.where(row_bit == col_bit, x, jnp.where(row_bit, down, up))
    return x


def kernel(
    wave_ref, pot_ref, proj_ref, kb_ref, atom_ref, corner_ref, out_ref,
    pbuf, halo, part_own, part_in, kb_own, kb_in, kb_pad, fields, boxes, acc, deposit_in,
    pick_z, pick_zt, pick_atom, pick_atom_t, band_z, cross, x_corner, local,
    gather_out, gather_in, halo_out, halo_in_sem, part_out_sem, part_in_sem, kb_out_sem, kb_in_sem,
):
    dom, band = lax.axis_index("dom"), lax.axis_index("band")
    doms = lax.axis_size("dom")
    y, z = lax.rem(band, Y_RING), lax.div(band, Y_RING)

    def dom_at(step):
        return lax.rem(dom + step + doms, doms)

    def band_at(dy, other):
        column = 1 - z if other else z
        return column * Y_RING + lax.rem(y + dy + Y_RING, Y_RING)

    gather_to = (band_at(1, False), band_at(-1, False), band_at(0, True))

    barrier = pltpu.get_barrier_semaphore()
    for target in gather_to:
        pl.semaphore_signal(barrier, inc=1, device_id=(dom, target), device_id_type=MESH)
    for step in REACHED:
        pl.semaphore_signal(barrier, inc=1, device_id=(dom_at(step), band), device_id_type=MESH)

    for p in range(PROJ):
        for g in range(4):
            x = proj_ref[pl.ds(64 * g + p, 8, stride=8), :]
            pbuf[band, p, :, pl.ds(128 * g, 128)] = transposed_parts(x)
    pad_rows = iota((128, 128), 0)
    kb_pad[...] = jnp.zeros((128, 128), F32)
    kb_pad[0:ATOM_DEV, 0:PROJ] = kb_ref[...]
    kb_own[...] = jnp.transpose(kb_pad[...])[0:8, :]

    pl.semaphore_wait(barrier, 3 + len(REACHED))

    def piece(way, n, owner, part):
        ref = pbuf.at[owner, pl.ds(part * PROJ_PART, PROJ_PART)]
        return pltpu.make_async_remote_copy(
            src_ref=ref, dst_ref=ref, send_sem=gather_out.at[way, n], recv_sem=gather_in.at[way, n],
            device_id=(dom, gather_to[way]), device_id_type=MESH,
        )

    sent = []

    def send(way, n, owner, part):
        copy = piece(way, n, owner, part)
        copy.start()
        sent.append(copy)

    def received(way, n, owner, part):
        piece(way, n, owner, part).wait_recv()

    for part in range(PARTS):
        for way in range(3):
            send(way, part, band, part)

    def halo_copy(app, side, source):
        planes = pl.ds(CX - REACH, REACH) if side == 0 else pl.ds(0, REACH)
        return pltpu.make_async_remote_copy(
            src_ref=source.at[planes], dst_ref=halo.at[app, side],
            send_sem=halo_out.at[app, side], recv_sem=halo_in_sem.at[app, side],
            device_id=(dom_at(1 if side == 0 else -1), band), device_id_type=MESH,
        )

    def part_copy(app, n):
        return pltpu.make_async_remote_copy(
            src_ref=part_own.at[app], dst_ref=part_in.at[app, n],
            send_sem=part_out_sem.at[app, n], recv_sem=part_in_sem.at[app, n],
            device_id=(dom_at(REACHED[n]), band), device_id_type=MESH,
        )

    def kb_copy(n):
        return pltpu.make_async_remote_copy(
            src_ref=kb_own, dst_ref=kb_in.at[n], send_sem=kb_out_sem.at[n], recv_sem=kb_in_sem.at[n],
            device_id=(dom_at(1 if n == 0 else -1), band), device_id_type=MESH,
        )

    def field(app):
        return wave_ref.at[0] if app == 0 else fields.at[app - 1]

    for n in range(2):
        kb_copy(n).start()
    for side in range(2):
        halo_copy(0, side, field(0)).start()

    lane = iota((8, 128), 1)
    lane_slot, lane_cell = lane >> 4, lane & 15
    first_atom = (dom - 1) * ATOM_DEV
    for g in range(4):
        at_x, at_z, atom = (jnp.zeros((8, 128), jnp.int32) for _ in range(3))
        for q in range(8):
            here = lane_slot == q
            at_x = jnp.where(here, corner_ref[0, 8 * g + q], at_x)
            at_z = jnp.where(here, corner_ref[2, 8 * g + q], at_z)
            atom = jnp.where(here, atom_ref[8 * g + q] - first_atom, atom)
        lanes = pl.ds(128 * g, 128)
        x_corner[:, lanes] = at_x
        hot_z = jnp.where(pad_rows == (at_z + lane_cell)[0:1, :], F32(1.0), F32(0.0))
        pick_z[:, lanes] = hot_z.astype(BF16)
        pick_zt[lanes, :] = jnp.transpose(hot_z).astype(BF16)
        hot_atom = jnp.where(pad_rows == atom[0:1, :], F32(1.0), F32(0.0))
        pick_atom[:, lanes] = hot_atom.astype(BF16)
        pick_atom_t[lanes, :] = jnp.transpose(hot_atom).astype(BF16)

    def extract(app):
        rows = field(app)[...].reshape(ROWS, CZ)
        high, low = split(rows)
        for g in range(4):
            lanes = pl.ds(128 * g, 128)
            hot = pick_z[:, lanes]
            along_z = (dot(high, hot) + dot(low, hot)).reshape(CX, CY, 128)
            at_x = x_corner[:, lanes][None, 0:1, :]
            cut = along_z[0:SX]
            for d in range(1, CX - SX + 1):
                cut = jnp.where(at_x == d, along_z[d : d + SX], cut)
            boxes[:, :, lanes] = cut.reshape(2 * SX, 8, 128)

    extract(0)

    distance = jnp.abs(iota((CZ, CZ), 0) - iota((CZ, CZ), 1))
    band_z[:, 0:128], band_z[:, 128:256] = split(weight_at(distance, 3.0 * KINETIC[0]))
    row, col = iota((ROWS, ROWS), 0), iota((ROWS, ROWS), 1)
    gap_x, gap_y = jnp.abs((row >> 4) - (col >> 4)), jnp.abs((row & 15) - (col & 15))
    gap = jnp.where(gap_x == 0, gap_y, jnp.where(gap_y == 0, gap_x, 99))
    cross[0:ROWS, :], cross[ROWS:, :] = split(weight_at(gap, 0.0))
    acc[...] = jnp.zeros((PROJ, 8, LANES), F32)

    def accumulate(owner, part):
        here = pl.ds(part * PROJ_PART, PROJ_PART)
        acc[here] = acc[here] + pbuf[owner, here] * boxes[owner][None]

    def apply_local(app):
        rows = field(app)[...].reshape(ROWS, CZ)
        high, low = split(rows)
        weights = band_z[...]
        both = dot(high, weights)
        out = both[:, 0:128] + both[:, 128:256] + dot(low, weights[:, 0:128])
        both = dot(cross[...], jnp.concatenate([high, low], axis=1))
        out = out + (both[0:ROWS, 0:128] + both[0:ROWS, 128:256] + both[ROWS:, 0:128])
        out = out + pot_ref[...].reshape(ROWS, CZ) * rows
        local[...] = out.reshape(CX, CY, CZ)

    def add_halo(app):
        for side in range(2):
            halo_copy(app, side, field(app)).wait_recv()
        low = jnp.where(dom > 0, halo[app, 0], F32(0.0))
        high = jnp.where(dom < doms - 1, halo[app, 1], F32(0.0))
        for x in range(REACH):
            local[x] = local[x] + sum(F32(KINETIC[k]) * low[REACH + x - k] for k in range(x + 1, REACH + 1))
            at = CX - 1 - x
            local[at] = local[at] + sum(F32(KINETIC[k]) * high[k - 1 - x] for k in range(x + 1, REACH + 1))

    both_halves = tuple(range(PARTS))
    first_half, last_half = both_halves[:HALF], both_halves[HALF:]

    for part in both_halves:
        accumulate(band, part)
    z_next = PARTS
    z_expected = [(band_at(0, True), part) for part in both_halves]
    for step in range(1, 5):
        arrived = []
        for part in both_halves:
            for way, sign in ((0, -1), (1, 1)):
                if step == 4 and part not in (first_half, last_half)[way]:
                    continue
                owner = band_at(sign * step, False)
                n = (step - 1) * PARTS + (part if step < 4 or way == 0 else part - HALF)
                received(way, n, owner, part)
                if step < 3:
                    send(way, step * PARTS + part, owner, part)
                elif step == 3 and part in (first_half, last_half)[way]:
                    send(way, 3 * PARTS + part - (0 if way == 0 else HALF), owner, part)
                if part in last_half or step == 4:
                    send(2, z_next, owner, part)
                    z_expected.append((band_at(sign * step, True), part))
                    z_next += 1
                arrived.append((owner, part))
        other_base = 3 * PARTS + HALF
        if step == 1:
            for part in both_halves:
                owner = band_at(0, True)
                received(2, part, owner, part)
                if part in first_half:
                    for way in range(2):
                        send(way, other_base + part, owner, part)
                arrived.append((owner, part))
        else:
            for part in first_half:
                for way, sign in ((0, -1), (1, 1)):
                    owner = band_at(sign * (step - 1), True)
                    n = other_base + (step - 2) * HALF + part
                    received(way, n, owner, part)
                    if step < 4:
                        send(way, n + HALF, owner, part)
                    arrived.append((owner, part))
        for owner, part in arrived:
            accumulate(owner, part)
        if step == 1:
            apply_local(0)
    for n in range(PARTS, SENDS):
        owner, part = z_expected[n]
        received(2, n, owner, part)
        accumulate(owner, part)

    for n in range(2):
        kb_copy(n).wait_recv()
    atom_lane = iota((8, 128), 1)
    energy = jnp.where(
        atom_lane < ATOM_DEV,
        kb_in[0],
        jnp.where(
            atom_lane < 2 * ATOM_DEV,
            pltpu.roll(kb_own[...], ATOM_DEV, 1),
            jnp.where(atom_lane < 3 * ATOM_DEV, pltpu.roll(kb_in[1], 2 * ATOM_DEV, 1), F32(0.0)),
        ),
    )
    centre, coefs = coefficients()
    for app in range(DEGREE):
        if app:
            extract(app)
            for g in range(4):
                lanes = pl.ds(128 * g, 128)
                total = pbuf[0, :, :, lanes] * boxes[0, :, lanes][None]
                for owner in range(1, 2 * SX):
                    total = total + pbuf[owner, :, :, lanes] * boxes[owner, :, lanes][None]
                acc[:, :, lanes] = total
        high, low = split(acc[...].reshape(PROJ * 8, LANES))
        hot = pick_atom_t[...]
        sums = (dot(high, hot) + dot(low, hot)).reshape(PROJ, 8, 128)
        part_own[app] = jnp.sum(sums, axis=1)
        for n in range(len(REACHED)):
            part_copy(app, n).start()
        if app:
            apply_local(app)
        add_halo(app)
        total = part_own[app]
        for n, step in enumerate(REACHED):
            part_copy(app, n).wait_recv()
            inside = (dom - step >= 0) & (dom - step < doms)
            shifted = pltpu.roll(part_in[app, n], (-step * ATOM_DEV) % 128, 1)
            total = total + jnp.where(inside, shifted, F32(0.0))
        high, low = split(total * energy)
        for g in range(4):
            lanes = pl.ds(128 * g, 128)
            hot = pick_atom[:, lanes]
            back = dot(high, hot) + dot(low, hot)
            weights = [jnp.broadcast_to(back[p : p + 1, :], (8, 128)) for p in range(PROJ)]
            at_x = x_corner[:, lanes]
            for half in range(2):
                values = []
                for i in range(SX):
                    value = pbuf[2 * i + half, 0, :, lanes] * weights[0]
                    for p in range(1, PROJ):
                        value = value + pbuf[2 * i + half, p, :, lanes] * weights[p]
                    values.append(value)
                for x in range(CX):
                    spread = jnp.zeros((8, 128), F32)
                    for d in range(max(0, x - SX + 1), min(x, CX - SX) + 1):
                        spread = jnp.where(at_x == d, values[x - d], spread)
                    deposit_in[pl.ds(x * CY + 8 * half, 8), lanes] = spread
        high, low = split(deposit_in[...])
        hot = pick_zt[...]
        nonlocal_part = (dot(high, hot) + dot(low, hot)).reshape(CX, CY, CZ)
        now = field(app)[...]
        scale, keep = coefs[app]
        new = F32(scale) * (local[...] + nonlocal_part - F32(centre) * now)
        if app:
            new = new - F32(keep) * field(app - 1)[...]
        if app < DEGREE - 1:
            fields[app] = new
            for side in range(2):
                halo_copy(app + 1, side, field(app + 1)).start()
        else:
            out_ref[0] = new

    for copy in sent:
        copy.wait_send()
    for n in range(2):
        kb_copy(n).wait_send()
    for app in range(DEGREE):
        for side in range(2):
            halo_copy(app, side, field(app)).wait_send()
        for n in range(len(REACHED)):
            part_copy(app, n).wait_send()


def on_device(wave_block, potential, projectors, kb_energy, slot_atom, slot_corner):
    vmem, smem = pl.BlockSpec(memory_space=pltpu.VMEM), pl.BlockSpec(memory_space=pltpu.SMEM)
    dma = pltpu.SemaphoreType.DMA
    return pl.pallas_call(
        kernel,
        out_shape=jax.ShapeDtypeStruct(wave_block.shape, F32),
        in_specs=[vmem, vmem, vmem, vmem, smem, smem],
        out_specs=vmem,
        scratch_shapes=[
            pltpu.VMEM((2 * SX, PROJ, 8, LANES), F32),
            pltpu.VMEM((DEGREE, 2, REACH, CY, CZ), F32),
            pltpu.VMEM((DEGREE, 8, 128), F32),
            pltpu.VMEM((DEGREE, len(REACHED), 8, 128), F32),
            pltpu.VMEM((8, 128), F32),
            pltpu.VMEM((2, 8, 128), F32),
            pltpu.VMEM((128, 128), F32),
            pltpu.VMEM((DEGREE - 1, CX, CY, CZ), F32),
            pltpu.VMEM((2 * SX, 8, LANES), F32),
            pltpu.VMEM((PROJ, 8, LANES), F32),
            pltpu.VMEM((ROWS, LANES), F32),
            pltpu.VMEM((CZ, LANES), BF16),
            pltpu.VMEM((LANES, CZ), BF16),
            pltpu.VMEM((128, LANES), BF16),
            pltpu.VMEM((LANES, 128), BF16),
            pltpu.VMEM((CZ, 256), BF16),
            pltpu.VMEM((2 * ROWS, ROWS), BF16),
            pltpu.VMEM((8, LANES), jnp.int32),
            pltpu.VMEM((CX, CY, CZ), F32),
            dma((3, SENDS)),
            dma((3, SENDS)),
            dma((DEGREE, 2)),
            dma((DEGREE, 2)),
            dma((DEGREE, len(REACHED))),
            dma((DEGREE, len(REACHED))),
            dma((2,)),
            dma((2,)),
        ],
        compiler_params=pltpu.CompilerParams(
            collective_id=0, has_side_effects=True, vmem_limit_bytes=32 * 1024 * 1024
        ),
        name="chebyshev",
    )(wave_block, potential, projectors.reshape(SLOTS * PROJ, 128), kb_energy, slot_atom, slot_corner)


def solution(mesh):
    placed = (
        P("band", "dom", None, None),
        P("dom", None, None),
        P("dom", None, "band"),
        P("dom", None),
        P("dom"),
        P(None, "dom"),
    )
    return jax.shard_map(
        on_device,
        mesh=mesh,
        in_specs=placed,
        out_specs=P("band", "dom", None, None),
        check_vma=False,
    )
```

```python
import jax
import jax.numpy as jnp
from jax import lax
from jax.experimental import pallas as pl
from jax.experimental.pallas import tpu as pltpu
from jax.sharding import PartitionSpec as P

SX, SY, SZ, DEGREE, PROJ = 8, 16, 16, 3, 8
CX, CY, CZ = 12, 16, 128
SLOTS, ATOM_DEV = 32, 16
LANES = SLOTS * SZ
ROWS = CX * CY
REACH = 6
Y_RING = 8
PARTS = 4
HALF = PARTS // 2
PROJ_PART = PROJ // PARTS
SENDS = 5 * PARTS
STENCIL = (
    -5369.0 / 1800.0,
    12.0 / 7.0,
    -15.0 / 56.0,
    10.0 / 189.0,
    -1.0 / 112.0,
    2.0 / 1925.0,
    -1.0 / 16632.0,
)
KINETIC = tuple(-0.5 * weight for weight in STENCIL)
LOWER_EDGE, UPPER_EDGE, ANCHOR_POINT = 3.0, 30.0, 0.5
F32, BF16 = jnp.float32, jnp.bfloat16
MESH = pl.DeviceIdType.MESH
REACHED = (1, 2, -1, -2)


def split(x):
    high = x.astype(BF16)
    return high, (x - high.astype(F32)).astype(BF16)


def dot(a, b):
    return jnp.dot(a, b, preferred_element_type=F32)


def iota(shape, dim):
    return lax.broadcasted_iota(jnp.int32, shape, dim)


def weight_at(distance, centre):
    out = jnp.where(distance == 0, F32(centre), F32(0.0))
    for k in range(1, REACH + 1):
        out = jnp.where(distance == k, F32(KINETIC[k]), out)
    return out


def coefficients():
    half_width = (UPPER_EDGE - LOWER_EDGE) / 2.0
    centre = (UPPER_EDGE + LOWER_EDGE) / 2.0
    sigma_first = half_width / (ANCHOR_POINT - centre)
    out = [(sigma_first / half_width, 0.0)]
    sigma = sigma_first
    for _ in range(2, DEGREE + 1):
        following = 1.0 / (2.0 / sigma_first - sigma)
        out.append((2.0 * following / half_width, sigma * following))
        sigma = following
    return centre, out


def transposed_parts(x):
    row, col = iota((8, 128), 0), iota((8, 128), 1) >> 4
    for bit in (1, 2, 4):
        row_bit, col_bit = (row & bit) != 0, (col & bit) != 0
        down = pltpu.roll(pltpu.roll(x, bit, 0), 128 - 16 * bit, 1)
        up = pltpu.roll(pltpu.roll(x, 8 - bit, 0), 16 * bit, 1)
        x = jnp.where(row_bit == col_bit, x, jnp.where(row_bit, down, up))
    return x


def kernel(
    wave_hbm, pot_hbm, proj_hbm, kb_hbm, atom_hbm, corner_hbm, out_ref,
    wave_ref, pot_ref, proj_ref, kb_fetched, atom_ref, corner_ref, fetched,
    pbuf, halo, part_own, part_in, kb_own, kb_in, fields, boxes, acc, deposit_in,
    pick_z, pick_zt, pick_atom, pick_atom_t, band_z, cross, x_corner, local,
    gather_out, gather_in, halo_out, halo_in_sem, part_out_sem, part_in_sem, kb_out_sem, kb_in_sem,
):
    dom, band = lax.axis_index("dom"), lax.axis_index("band")
    doms = lax.axis_size("dom")
    y, z = lax.rem(band, Y_RING), lax.div(band, Y_RING)

    def dom_at(step):
        return lax.rem(dom + step + doms, doms)

    def band_at(dy, other):
        column = 1 - z if other else z
        return column * Y_RING + lax.rem(y + dy + Y_RING, Y_RING)

    gather_to = (band_at(1, False), band_at(-1, False), band_at(0, True))

    kb_own[...] = jnp.zeros((8, 128), F32)
    fetches = [
        pltpu.make_async_copy(source, target, fetched.at[n])
        for n, (source, target) in enumerate(
            (
                (proj_hbm, proj_ref),
                (wave_hbm.at[0], wave_ref),
                (corner_hbm, corner_ref),
                (atom_hbm, atom_ref),
                (kb_hbm, kb_fetched),
                (pot_hbm, pot_ref),
            )
        )
    ]
    for fetch in fetches:
        fetch.start()

    barrier = pltpu.get_barrier_semaphore()
    for target in gather_to:
        pl.semaphore_signal(barrier, inc=1, device_id=(dom, target), device_id_type=MESH)
    for step in REACHED:
        pl.semaphore_signal(barrier, inc=1, device_id=(dom_at(step), band), device_id_type=MESH)

    def piece(way, n, owner, part):
        ref = pbuf.at[owner, pl.ds(part * PROJ_PART, PROJ_PART)]
        return pltpu.make_async_remote_copy(
            src_ref=ref, dst_ref=ref, send_sem=gather_out.at[way, n], recv_sem=gather_in.at[way, n],
            device_id=(dom, gather_to[way]), device_id_type=MESH,
        )

    sent = []

    def send(way, n, owner, part):
        copy = piece(way, n, owner, part)
        copy.start()
        sent.append(copy)

    def received(way, n, owner, part):
        piece(way, n, owner, part).wait_recv()

    fetches[0].wait()
    for part in range(PARTS):
        for p in range(part * PROJ_PART, (part + 1) * PROJ_PART):
            for g in range(4):
                x = proj_ref[pl.ds(64 * g + p, 8, stride=8), :]
                pbuf[band, p, :, pl.ds(128 * g, 128)] = transposed_parts(x)
        if part == 0:
            pl.semaphore_wait(barrier, 3 + len(REACHED))
        for way in range(3):
            send(way, part, band, part)

    def halo_copy(app, side, source):
        planes = pl.ds(CX - REACH, REACH) if side == 0 else pl.ds(0, REACH)
        return pltpu.make_async_remote_copy(
            src_ref=source.at[planes], dst_ref=halo.at[app, side],
            send_sem=halo_out.at[app, side], recv_sem=halo_in_sem.at[app, side],
            device_id=(dom_at(1 if side == 0 else -1), band), device_id_type=MESH,
        )

    def part_copy(app, n):
        return pltpu.make_async_remote_copy(
            src_ref=part_own.at[app], dst_ref=part_in.at[app, n],
            send_sem=part_out_sem.at[app, n], recv_sem=part_in_sem.at[app, n],
            device_id=(dom_at(REACHED[n]), band), device_id_type=MESH,
        )

    def kb_copy(n):
        return pltpu.make_async_remote_copy(
            src_ref=kb_own, dst_ref=kb_in.at[n], send_sem=kb_out_sem.at[n], recv_sem=kb_in_sem.at[n],
            device_id=(dom_at(1 if n == 0 else -1), band), device_id_type=MESH,
        )

    def field(app):
        return wave_ref if app == 0 else fields.at[app - 1]

    for fetch in fetches[1:]:
        fetch.wait()
    kb_own[:, 0:ATOM_DEV] = kb_fetched[...]
    for n in range(2):
        kb_copy(n).start()
    for side in range(2):
        halo_copy(0, side, field(0)).start()

    lane = iota((8, 128), 1)
    lane_slot, lane_cell = lane >> 4, lane & 15
    pad_rows = iota((128, 128), 0)
    first_atom = (dom - 1) * ATOM_DEV
    for g in range(4):
        at_x, at_z, atom = (jnp.zeros((8, 128), jnp.int32) for _ in range(3))
        for q in range(8):
            here = lane_slot == q
            at_x = jnp.where(here, corner_ref[0, 8 * g + q], at_x)
            at_z = jnp.where(here, corner_ref[2, 8 * g + q], at_z)
            atom = jnp.where(here, atom_ref[8 * g + q] - first_atom, atom)
        lanes = pl.ds(128 * g, 128)
        x_corner[:, lanes] = at_x
        hot_z = jnp.where(pad_rows == (at_z + lane_cell)[0:1, :], F32(1.0), F32(0.0))
        pick_z[:, lanes] = hot_z.astype(BF16)
        pick_zt[lanes, :] = jnp.transpose(hot_z).astype(BF16)
        hot_atom = jnp.where(pad_rows == atom[0:1, :], F32(1.0), F32(0.0))
        pick_atom[:, lanes] = hot_atom.astype(BF16)
        pick_atom_t[lanes, :] = jnp.transpose(hot_atom).astype(BF16)

    def extract(app):
        rows = field(app)[...].reshape(ROWS, CZ)
        high, low = split(rows)
        for g in range(4):
            lanes = pl.ds(128 * g, 128)
            hot = pick_z[:, lanes]
            along_z = (dot(high, hot) + dot(low, hot)).reshape(CX, CY, 128)
            at_x = x_corner[:, lanes][None, 0:1, :]
            cut = along_z[0:SX]
            for d in range(1, CX - SX + 1):
                cut = jnp.where(at_x == d, along_z[d : d + SX], cut)
            boxes[:, :, lanes] = cut.reshape(2 * SX, 8, 128)

    extract(0)

    distance = jnp.abs(iota((CZ, CZ), 0) - iota((CZ, CZ), 1))
    band_z[:, 0:128], band_z[:, 128:256] = split(weight_at(distance, 3.0 * KINETIC[0]))
    row, col = iota((ROWS, ROWS), 0), iota((ROWS, ROWS), 1)
    gap_x, gap_y = jnp.abs((row >> 4) - (col >> 4)), jnp.abs((row & 15) - (col & 15))
    gap = jnp.where(gap_x == 0, gap_y, jnp.where(gap_y == 0, gap_x, 99))
    cross[0:ROWS, :], cross[ROWS:, :] = split(weight_at(gap, 0.0))
    acc[...] = jnp.zeros((PROJ, 8, LANES), F32)

    def accumulate(owner, part):
        here = pl.ds(part * PROJ_PART, PROJ_PART)
        acc[here] = acc[here] + pbuf[owner, here] * boxes[owner][None]

    def apply_local(app):
        rows = field(app)[...].reshape(ROWS, CZ)
        high, low = split(rows)
        weights = band_z[...]
        both = dot(high, weights)
        out = both[:, 0:128] + both[:, 128:256] + dot(low, weights[:, 0:128])
        both = dot(cross[...], jnp.concatenate([high, low], axis=1))
        out = out + (both[0:ROWS, 0:128] + both[0:ROWS, 128:256] + both[ROWS:, 0:128])
        out = out + pot_ref[...].reshape(ROWS, CZ) * rows
        local[...] = out.reshape(CX, CY, CZ)

    def add_halo(app):
        for side in range(2):
            halo_copy(app, side, field(app)).wait_recv()
        low = jnp.where(dom > 0, halo[app, 0], F32(0.0))
        high = jnp.where(dom < doms - 1, halo[app, 1], F32(0.0))
        for x in range(REACH):
            local[x] = local[x] + sum(F32(KINETIC[k]) * low[REACH + x - k] for k in range(x + 1, REACH + 1))
            at = CX - 1 - x
            local[at] = local[at] + sum(F32(KINETIC[k]) * high[k - 1 - x] for k in range(x + 1, REACH + 1))

    both_halves = tuple(range(PARTS))
    first_half, last_half = both_halves[:HALF], both_halves[HALF:]

    for part in both_halves:
        accumulate(band, part)
    z_next = PARTS
    z_expected = [(band_at(0, True), part) for part in both_halves]
    for step in range(1, 5):
        arrived = []
        for part in both_halves:
            for way, sign in ((0, -1), (1, 1)):
                if step == 4 and part not in (first_half, last_half)[way]:
                    continue
                owner = band_at(sign * step, False)
                n = (step - 1) * PARTS + (part if step < 4 or way == 0 else part - HALF)
                received(way, n, owner, part)
                if step < 3:
                    send(way, step * PARTS + part, owner, part)
                elif step == 3 and part in (first_half, last_half)[way]:
                    send(way, 3 * PARTS + part - (0 if way == 0 else HALF), owner, part)
                if part in last_half or step == 4:
                    send(2, z_next, owner, part)
                    z_expected.append((band_at(sign * step, True), part))
                    z_next += 1
                arrived.append((owner, part))
        other_base = 3 * PARTS + HALF
        if step == 1:
            for part in both_halves:
                owner = band_at(0, True)
                received(2, part, owner, part)
                if part in first_half:
                    for way in range(2):
                        send(way, other_base + part, owner, part)
                arrived.append((owner, part))
        else:
            for part in first_half:
                for way, sign in ((0, -1), (1, 1)):
                    owner = band_at(sign * (step - 1), True)
                    n = other_base + (step - 2) * HALF + part
                    received(way, n, owner, part)
                    if step < 4:
                        send(way, n + HALF, owner, part)
                    arrived.append((owner, part))
        for owner, part in arrived:
            accumulate(owner, part)
        if step == 1:
            apply_local(0)
    for n in range(PARTS, SENDS):
        owner, part = z_expected[n]
        received(2, n, owner, part)
        accumulate(owner, part)

    for n in range(2):
        kb_copy(n).wait_recv()
    atom_lane = iota((8, 128), 1)
    energy = jnp.where(
        atom_lane < ATOM_DEV,
        kb_in[0],
        jnp.where(
            atom_lane < 2 * ATOM_DEV,
            pltpu.roll(kb_own[...], ATOM_DEV, 1),
            jnp.where(atom_lane < 3 * ATOM_DEV, pltpu.roll(kb_in[1], 2 * ATOM_DEV, 1), F32(0.0)),
        ),
    )
    centre, coefs = coefficients()
    for app in range(DEGREE):
        if app:
            extract(app)
            for g in range(4):
                lanes = pl.ds(128 * g, 128)
                total = pbuf[0, :, :, lanes] * boxes[0, :, lanes][None]
                for owner in range(1, 2 * SX):
                    total = total + pbuf[owner, :, :, lanes] * boxes[owner, :, lanes][None]
                acc[:, :, lanes] = total
        high, low = split(acc[...].reshape(PROJ * 8, LANES))
        hot = pick_atom_t[...]
        sums = (dot(high, hot) + dot(low, hot)).reshape(PROJ, 8, 128)
        part_own[app] = jnp.sum(sums, axis=1)
        for n in range(len(REACHED)):
            part_copy(app, n).start()
        if app:
            apply_local(app)
        add_halo(app)
        total = part_own[app]
        for n, step in enumerate(REACHED):
            part_copy(app, n).wait_recv()
            inside = (dom - step >= 0) & (dom - step < doms)
            shifted = pltpu.roll(part_in[app, n], (-step * ATOM_DEV) % 128, 1)
            total = total + jnp.where(inside, shifted, F32(0.0))
        high, low = split(total * energy)
        for g in range(4):
            lanes = pl.ds(128 * g, 128)
            hot = pick_atom[:, lanes]
            back = dot(high, hot) + dot(low, hot)
            weights = [jnp.broadcast_to(back[p : p + 1, :], (8, 128)) for p in range(PROJ)]
            at_x = x_corner[:, lanes]
            for half in range(2):
                values = []
                for i in range(SX):
                    value = pbuf[2 * i + half, 0, :, lanes] * weights[0]
                    for p in range(1, PROJ):
                        value = value + pbuf[2 * i + half, p, :, lanes] * weights[p]
                    values.append(value)
                for x in range(CX):
                    spread = jnp.zeros((8, 128), F32)
                    for d in range(max(0, x - SX + 1), min(x, CX - SX) + 1):
                        spread = jnp.where(at_x == d, values[x - d], spread)
                    deposit_in[pl.ds(x * CY + 8 * half, 8), lanes] = spread
        high, low = split(deposit_in[...])
        hot = pick_zt[...]
        nonlocal_part = (dot(high, hot) + dot(low, hot)).reshape(CX, CY, CZ)
        now = field(app)[...]
        scale, keep = coefs[app]
        new = F32(scale) * (local[...] + nonlocal_part - F32(centre) * now)
        if app:
            new = new - F32(keep) * field(app - 1)[...]
        if app < DEGREE - 1:
            fields[app] = new
            for side in range(2):
                halo_copy(app + 1, side, field(app + 1)).start()
        else:
            out_ref[0] = new

    for copy in sent:
        copy.wait_send()
    for n in range(2):
        kb_copy(n).wait_send()
    for app in range(DEGREE):
        for side in range(2):
            halo_copy(app, side, field(app)).wait_send()
        for n in range(len(REACHED)):
            part_copy(app, n).wait_send()


def on_device(wave_block, potential, projectors, kb_energy, slot_atom, slot_corner):
    vmem, hbm = pl.BlockSpec(memory_space=pltpu.VMEM), pl.BlockSpec(memory_space=pltpu.HBM)
    dma = pltpu.SemaphoreType.DMA
    return pl.pallas_call(
        kernel,
        out_shape=jax.ShapeDtypeStruct(wave_block.shape, F32),
        in_specs=[hbm] * 6,
        out_specs=vmem,
        scratch_shapes=[
            pltpu.VMEM((CX, CY, CZ), F32),
            pltpu.VMEM((CX, CY, CZ), F32),
            pltpu.VMEM((SLOTS * PROJ, 128), F32),
            pltpu.VMEM((8, ATOM_DEV), F32),
            pltpu.SMEM((SLOTS,), jnp.int32),
            pltpu.SMEM((3, SLOTS), jnp.int32),
            dma((6,)),
            pltpu.VMEM((2 * SX, PROJ, 8, LANES), F32),
            pltpu.VMEM((DEGREE, 2, REACH, CY, CZ), F32),
            pltpu.VMEM((DEGREE, 8, 128), F32),
            pltpu.VMEM((DEGREE, len(REACHED), 8, 128), F32),
            pltpu.VMEM((8, 128), F32),
            pltpu.VMEM((2, 8, 128), F32),
            pltpu.VMEM((DEGREE - 1, CX, CY, CZ), F32),
            pltpu.VMEM((2 * SX, 8, LANES), F32),
            pltpu.VMEM((PROJ, 8, LANES), F32),
            pltpu.VMEM((ROWS, LANES), F32),
            pltpu.VMEM((CZ, LANES), BF16),
            pltpu.VMEM((LANES, CZ), BF16),
            pltpu.VMEM((128, LANES), BF16),
            pltpu.VMEM((LANES, 128), BF16),
            pltpu.VMEM((CZ, 256), BF16),
            pltpu.VMEM((2 * ROWS, ROWS), BF16),
            pltpu.VMEM((8, LANES), jnp.int32),
            pltpu.VMEM((CX, CY, CZ), F32),
            dma((3, SENDS)),
            dma((3, SENDS)),
            dma((DEGREE, 2)),
            dma((DEGREE, 2)),
            dma((DEGREE, len(REACHED))),
            dma((DEGREE, len(REACHED))),
            dma((2,)),
            dma((2,)),
        ],
        compiler_params=pltpu.CompilerParams(
            collective_id=0, has_side_effects=True, vmem_limit_bytes=60 * 1024 * 1024
        ),
        name="chebyshev",
    )(wave_block, potential, projectors.reshape(SLOTS * PROJ, 128), kb_energy.T, slot_atom, slot_corner)


def solution(mesh):
    placed = (
        P("band", "dom", None, None),
        P("dom", None, None),
        P("dom", None, "band"),
        P("dom", None),
        P("dom"),
        P(None, "dom"),
    )
    return jax.shard_map(
        on_device,
        mesh=mesh,
        in_specs=placed,
        out_specs=P("band", "dom", None, None),
        check_vma=False,
    )
```

```python
import functools

import jax
import jax.numpy as jnp
from jax import lax
from jax.experimental import pallas as pl
from jax.experimental.pallas import tpu as pltpu
from jax.sharding import PartitionSpec as P

SX, SY, SZ, DEGREE, PROJ = 8, 16, 16, 3, 8
CX, CY, CZ = 12, 16, 128
SLOTS, ATOM_DEV = 32, 16
LANES = SLOTS * SZ
ROWS = CX * CY
REACH = 6
Y_RING = 8
PARTS = 4
HALF = PARTS // 2
PROJ_PART = PROJ // PARTS
RING_PARTS = (2, 2, 2)
RING_SENDS = 3 * PARTS + HALF + sum(RING_PARTS)
Z_SENDS = 2 * PARTS + 2 * sum(PARTS - count for count in RING_PARTS)
SENDS = max(RING_SENDS, Z_SENDS)
STENCIL = (
    -5369.0 / 1800.0,
    12.0 / 7.0,
    -15.0 / 56.0,
    10.0 / 189.0,
    -1.0 / 112.0,
    2.0 / 1925.0,
    -1.0 / 16632.0,
)
KINETIC = tuple(-0.5 * weight for weight in STENCIL)
LOWER_EDGE, UPPER_EDGE, ANCHOR_POINT = 3.0, 30.0, 0.5
F32, BF16 = jnp.float32, jnp.bfloat16
MESH = pl.DeviceIdType.MESH
REACHED = (1, 2, -1, -2)
REACHED_BY_MATE = (0,) + REACHED
SIDES = (1, -1)


def split(x):
    high = x.astype(BF16)
    return high, (x - high.astype(F32)).astype(BF16)


def dot(a, b):
    return jnp.dot(a, b, preferred_element_type=F32)


def iota(shape, dim):
    return lax.broadcasted_iota(jnp.int32, shape, dim)


def weight_at(distance, centre):
    out = jnp.where(distance == 0, F32(centre), F32(0.0))
    for k in range(1, REACH + 1):
        out = jnp.where(distance == k, F32(KINETIC[k]), out)
    return out


def coefficients():
    half_width = (UPPER_EDGE - LOWER_EDGE) / 2.0
    centre = (UPPER_EDGE + LOWER_EDGE) / 2.0
    sigma_first = half_width / (ANCHOR_POINT - centre)
    out = [(sigma_first / half_width, 0.0)]
    sigma = sigma_first
    for _ in range(2, DEGREE + 1):
        following = 1.0 / (2.0 / sigma_first - sigma)
        out.append((2.0 * following / half_width, sigma * following))
        sigma = following
    return centre, out


def transposed_parts(x):
    row, col = iota((8, 128), 0), iota((8, 128), 1) >> 4
    for bit in (1, 2, 4):
        row_bit, col_bit = (row & bit) != 0, (col & bit) != 0
        down = pltpu.roll(pltpu.roll(x, bit, 0), 128 - 16 * bit, 1)
        up = pltpu.roll(pltpu.roll(x, 8 - bit, 0), 16 * bit, 1)
        x = jnp.where(row_bit == col_bit, x, jnp.where(row_bit, down, up))
    return x


def kernel(
    wave_hbm, pot_hbm, proj_hbm, kb_hbm, atom_hbm, corner_hbm, out_ref,
    wave_ref, pot_ref, proj_ref, kb_fetched, atom_ref, corner_ref, fetched,
    pbuf, halo, part_own, part_in, kb_own, kb_in, fields, boxes, acc, deposit_in,
    mate_field, mate_boxes, mate_acc, mate_part, mate_part_in,
    pick_z, pick_zt, pick_atom, pick_atom_t, band_z, cross, x_corner, local,
    gather_out, gather_in, mate_out_sem, mate_in_sem, halo_out, halo_in_sem, part_out_sem, part_in_sem, kb_out_sem, kb_in_sem,
):
    dom, band = lax.axis_index("dom"), lax.axis_index("band")
    doms = lax.axis_size("dom")
    y, z = lax.rem(band, Y_RING), lax.div(band, Y_RING)

    def inside(step):
        return (dom + step >= 0) & (dom + step < doms)

    def where_inside(step, work):
        pl.when(inside(step))(work)

    def band_at(dy, other):
        column = 1 - z if other else z
        return column * Y_RING + lax.rem(y + dy + Y_RING, Y_RING)

    gather_to = (band_at(1, False), band_at(-1, False), band_at(0, True))

    kb_own[...] = jnp.zeros((8, 128), F32)
    fetches = [
        pltpu.make_async_copy(source, target, fetched.at[n])
        for n, (source, target) in enumerate(
            (
                (proj_hbm, proj_ref),
                (wave_hbm.at[0], wave_ref),
                (corner_hbm, corner_ref),
                (atom_hbm, atom_ref),
                (kb_hbm, kb_fetched),
                (pot_hbm, pot_ref),
            )
        )
    ]
    for fetch in fetches:
        fetch.start()

    barrier = pltpu.get_barrier_semaphore()
    for target in gather_to:
        pl.semaphore_signal(barrier, inc=1, device_id=(dom, target), device_id_type=MESH)
    for step in REACHED:

        @functools.partial(where_inside, step)
        def _():
            for target in (band, gather_to[2]):
                pl.semaphore_signal(barrier, inc=1, device_id=(dom + step, target), device_id_type=MESH)

    def piece(way, n, owner, part):
        ref = pbuf.at[owner, pl.ds(part * PROJ_PART, PROJ_PART)]
        return pltpu.make_async_remote_copy(
            src_ref=ref, dst_ref=ref, send_sem=gather_out.at[way, n], recv_sem=gather_in.at[way, n],
            device_id=(dom, gather_to[way]), device_id_type=MESH,
        )

    sent = []

    def send(way, n, owner, part):
        copy = piece(way, n, owner, part)
        copy.start()
        sent.append(copy)

    def received(way, n, owner, part):
        piece(way, n, owner, part).wait_recv()

    fetches[0].wait()
    for part in range(PARTS):
        for p in range(part * PROJ_PART, (part + 1) * PROJ_PART):
            for g in range(4):
                x = proj_ref[pl.ds(64 * g + p, 8, stride=8), :]
                pbuf[band, p, :, pl.ds(128 * g, 128)] = transposed_parts(x)
        if part == 0:
            pl.semaphore_wait(barrier, 3 + 2 * sum(inside(step).astype(jnp.int32) for step in REACHED))
        for way in range(3):
            send(way, part, band, part)

    def halo_copy(app, side, source):
        planes = pl.ds(CX - REACH, REACH) if side == 0 else pl.ds(0, REACH)
        return pltpu.make_async_remote_copy(
            src_ref=source.at[planes], dst_ref=halo.at[app, side],
            send_sem=halo_out.at[app, side], recv_sem=halo_in_sem.at[app, side],
            device_id=(dom + (1 if side == 0 else -1), band), device_id_type=MESH,
        )

    def part_copy(app, n):
        return pltpu.make_async_remote_copy(
            src_ref=part_own.at[app], dst_ref=part_in.at[app, n],
            send_sem=part_out_sem.at[app, n], recv_sem=part_in_sem.at[app, n],
            device_id=(dom + REACHED[n], band), device_id_type=MESH,
        )

    def mate_copy():
        return pltpu.make_async_remote_copy(
            src_ref=wave_ref.at[pl.ds((SX // 2) * (1 - z), SX)], dst_ref=mate_field,
            send_sem=mate_out_sem.at[0], recv_sem=mate_in_sem.at[0],
            device_id=(dom, gather_to[2]), device_id_type=MESH,
        )

    def mate_part_copy(n):
        return pltpu.make_async_remote_copy(
            src_ref=mate_part, dst_ref=mate_part_in.at[n],
            send_sem=mate_out_sem.at[1 + n], recv_sem=mate_in_sem.at[1 + n],
            device_id=(dom + REACHED_BY_MATE[n], gather_to[2]), device_id_type=MESH,
        )

    def kb_copy(n):
        return pltpu.make_async_remote_copy(
            src_ref=kb_own, dst_ref=kb_in.at[n], send_sem=kb_out_sem.at[n], recv_sem=kb_in_sem.at[n],
            device_id=(dom + (1 if n == 0 else -1), band), device_id_type=MESH,
        )

    def field(app):
        return wave_ref if app == 0 else fields.at[app - 1]

    for fetch in fetches[1:]:
        fetch.wait()
    kb_own[:, 0:ATOM_DEV] = kb_fetched[...]
    mate_copy().start()
    for n in range(2):
        where_inside(SIDES[n], kb_copy(n).start)
    for side in range(2):
        where_inside(SIDES[side], halo_copy(0, side, field(0)).start)

    def make_picks():
        lane = iota((8, 128), 1)
        lane_slot, lane_cell = lane >> 4, lane & 15
        pad_rows = iota((128, 128), 0)
        first_atom = (dom - 1) * ATOM_DEV
        for g in range(4):
            at_x, at_z, atom = (jnp.zeros((8, 128), jnp.int32) for _ in range(3))
            for q in range(8):
                here = lane_slot == q
                at_x = jnp.where(here, corner_ref[0, 8 * g + q], at_x)
                at_z = jnp.where(here, corner_ref[2, 8 * g + q], at_z)
                atom = jnp.where(here, atom_ref[8 * g + q] - first_atom, atom)
            lanes = pl.ds(128 * g, 128)
            x_corner[:, lanes] = at_x
            hot_z = jnp.where(pad_rows == (at_z + lane_cell)[0:1, :], F32(1.0), F32(0.0))
            pick_z[:, lanes] = hot_z.astype(BF16)
            pick_zt[lanes, :] = jnp.transpose(hot_z).astype(BF16)
            hot_atom = jnp.where(pad_rows == atom[0:1, :], F32(1.0), F32(0.0))
            pick_atom[:, lanes] = hot_atom.astype(BF16)
            pick_atom_t[lanes, :] = jnp.transpose(hot_atom).astype(BF16)

    def extract(planes, out):
        count = out.shape[0] // 2
        extent = count + CX - SX
        high, low = split(planes[...].reshape(extent * CY, CZ))
        for g in range(4):
            lanes = pl.ds(128 * g, 128)
            hot = pick_z[:, lanes]
            along_z = (dot(high, hot) + dot(low, hot)).reshape(extent, CY, 128)
            at_x = x_corner[:, lanes][None, 0:1, :]
            cut = along_z[0:count]
            for d in range(1, CX - SX + 1):
                cut = jnp.where(at_x == d, along_z[d : d + count], cut)
            out[:, :, lanes] = cut.reshape(2 * count, 8, 128)

    def make_stencil():
        distance = jnp.abs(iota((CZ, CZ), 0) - iota((CZ, CZ), 1))
        band_z[:, 0:128], band_z[:, 128:256] = split(weight_at(distance, 3.0 * KINETIC[0]))
        row, col = iota((ROWS, ROWS), 0), iota((ROWS, ROWS), 1)
        gap_x, gap_y = jnp.abs((row >> 4) - (col >> 4)), jnp.abs((row & 15) - (col & 15))
        gap = jnp.where(gap_x == 0, gap_y, jnp.where(gap_y == 0, gap_x, 99))
        cross[0:ROWS, :], cross[ROWS:, :] = split(weight_at(gap, 0.0))

    def accumulate(step, part, own=True, mate=True):
        owner, at = band_at(step, False), lax.rem(y + step + Y_RING, Y_RING)
        here = pl.ds(part * PROJ_PART, PROJ_PART)
        values = pbuf[owner, here]
        for wanted, total, cells in ((own, acc, boxes[owner]), (mate, mate_acc, mate_boxes[at])):
            if wanted:
                term = values * cells[None]
                total[here] = term if step == 0 else total[here] + term

    def atom_partials(total):
        high, low = split(total[...].reshape(PROJ * 8, LANES))
        hot = pick_atom_t[...]
        return jnp.sum((dot(high, hot) + dot(low, hot)).reshape(PROJ, 8, 128), axis=1)

    def apply_local(app):
        rows = field(app)[...].reshape(ROWS, CZ)
        high, low = split(rows)
        weights = band_z[...]
        both = dot(high, weights)
        out = both[:, 0:128] + both[:, 128:256] + dot(low, weights[:, 0:128])
        both = dot(cross[...], jnp.concatenate([high, low], axis=1))
        out = out + (both[0:ROWS, 0:128] + both[0:ROWS, 128:256] + both[ROWS:, 0:128])
        out = out + pot_ref[...].reshape(ROWS, CZ) * rows
        local[...] = out.reshape(CX, CY, CZ)

    def add_halo(app):
        for side in range(2):
            where_inside(-SIDES[side], halo_copy(app, side, field(app)).wait_recv)
        low = jnp.where(dom > 0, halo[app, 0], F32(0.0))
        high = jnp.where(dom < doms - 1, halo[app, 1], F32(0.0))
        for x in range(REACH):
            local[x] = local[x] + sum(F32(KINETIC[k]) * low[REACH + x - k] for k in range(x + 1, REACH + 1))
            at = CX - 1 - x
            local[at] = local[at] + sum(F32(KINETIC[k]) * high[k - 1 - x] for k in range(x + 1, REACH + 1))

    all_parts = tuple(range(PARTS))
    halves = all_parts[:HALF], all_parts[HALF:]
    ways = ((0, -1), (1, 1))
    z_expected = [(band_at(0, True), part) for part in all_parts]
    z_waiting = []

    def to_mate(step, part):
        z_waiting.append((step, part))

    def flush_to_mate():
        for step, part in z_waiting:
            send(2, len(z_expected), band_at(step, False), part)
            z_expected.append((band_at(step, True), part))
        z_waiting.clear()

    def other_ring(hop, part):
        return 3 * PARTS + HALF + sum(RING_PARTS[:hop]) + part

    def pass_other(hop):
        for part in range(RING_PARTS[hop - 1] if hop else RING_PARTS[0]):
            for way, sign in ways:
                owner = band_at(sign * hop, True)
                if hop:
                    received(way, other_ring(hop - 1, part), owner, part)
                elif way == 0:
                    received(2, part, owner, part)
                if hop < 3 and part < RING_PARTS[hop]:
                    send(way, other_ring(hop, part), owner, part)

    for step in range(1, 4):
        for part in all_parts:
            for way, sign in ways:
                owner = band_at(sign * step, False)
                received(way, (step - 1) * PARTS + part, owner, part)
                if step < 3:
                    send(way, step * PARTS + part, owner, part)
                elif part in halves[way]:
                    send(way, 3 * PARTS + part - halves[way][0], owner, part)
                if part >= RING_PARTS[step - 1]:
                    to_mate(sign * step, part)
                    flush_to_mate()
        pass_other(step - 1)
        if step == 1:
            make_picks()
            extract(field(0), boxes)
            for part in all_parts:
                accumulate(0, part, mate=False)
                for sign in (-1, 1):
                    accumulate(sign, part, mate=False)
        elif step == 2:
            mate_copy().wait_recv()
            extract(mate_field, mate_boxes)
            for part in all_parts:
                accumulate(0, part, own=False)
                for sign in (-1, 1):
                    accumulate(sign, part, own=False)
                    accumulate(2 * sign, part)
        else:
            for part in all_parts:
                for sign in (-1, 1):
                    accumulate(3 * sign, part)
    for part in range(HALF):
        for way, sign in ways:
            at = halves[way][part]
            received(way, 3 * PARTS + part, band_at(4, False), at)
            to_mate(4, at)
            flush_to_mate()
            accumulate(4, at)
    part_own[0] = atom_partials(acc)
    mate_part[...] = atom_partials(mate_acc)
    for n in range(len(REACHED)):
        where_inside(REACHED[n], part_copy(0, n).start)
        where_inside(REACHED[n], mate_part_copy(n + 1).start)
    mate_part_copy(0).start()
    pass_other(3)
    make_stencil()
    apply_local(0)
    for n, (owner, part) in enumerate(z_expected):
        if n >= PARTS or part >= RING_PARTS[0]:
            received(2, n, owner, part)
    add_halo(0)

    for n in range(2):
        where_inside(-SIDES[n], kb_copy(n).wait_recv)
    atom_lane = iota((8, 128), 1)
    energy = jnp.where(
        atom_lane < ATOM_DEV,
        jnp.where(dom > 0, kb_in[0], F32(0.0)),
        jnp.where(
            atom_lane < 2 * ATOM_DEV,
            pltpu.roll(kb_own[...], ATOM_DEV, 1),
            jnp.where((atom_lane < 3 * ATOM_DEV) & (dom < doms - 1), pltpu.roll(kb_in[1], 2 * ATOM_DEV, 1), F32(0.0)),
        ),
    )
    centre, coefs = coefficients()
    for app in range(DEGREE):
        if app:
            extract(field(app), boxes)
            for g in range(4):
                lanes = pl.ds(128 * g, 128)
                total = pbuf[0, :, :, lanes] * boxes[0, :, lanes][None]
                for owner in range(1, 2 * SX):
                    total = total + pbuf[owner, :, :, lanes] * boxes[owner, :, lanes][None]
                acc[:, :, lanes] = total
            part_own[app] = atom_partials(acc)
            for n in range(len(REACHED)):
                where_inside(REACHED[n], part_copy(app, n).start)
            apply_local(app)
            add_halo(app)
        total = part_own[app]
        if app == 0:
            mate_part_copy(0).wait_recv()
            total = total + mate_part_in[0]
        for n, step in enumerate(REACHED):
            where_inside(-step, part_copy(app, n).wait_recv)
            partial = part_in[app, n]
            if app == 0:
                where_inside(-step, mate_part_copy(n + 1).wait_recv)
                partial = partial + mate_part_in[n + 1]
            shifted = pltpu.roll(partial, (-step * ATOM_DEV) % 128, 1)
            total = total + jnp.where(inside(-step), shifted, F32(0.0))
        high, low = split(total * energy)
        for g in range(4):
            lanes = pl.ds(128 * g, 128)
            hot = pick_atom[:, lanes]
            back = dot(high, hot) + dot(low, hot)
            weights = [jnp.broadcast_to(back[p : p + 1, :], (8, 128)) for p in range(PROJ)]
            at_x = x_corner[:, lanes]
            for half in range(2):
                values = []
                for i in range(SX):
                    value = pbuf[2 * i + half, 0, :, lanes] * weights[0]
                    for p in range(1, PROJ):
                        value = value + pbuf[2 * i + half, p, :, lanes] * weights[p]
                    values.append(value)
                for x in range(CX):
                    spread = jnp.zeros((8, 128), F32)
                    for d in range(max(0, x - SX + 1), min(x, CX - SX) + 1):
                        spread = jnp.where(at_x == d, values[x - d], spread)
                    deposit_in[pl.ds(x * CY + 8 * half, 8), lanes] = spread
        high, low = split(deposit_in[...])
        hot = pick_zt[...]
        nonlocal_part = (dot(high, hot) + dot(low, hot)).reshape(CX, CY, CZ)
        now = field(app)[...]
        scale, keep = coefs[app]
        new = F32(scale) * (local[...] + nonlocal_part - F32(centre) * now)
        if app:
            new = new - F32(keep) * field(app - 1)[...]
        if app < DEGREE - 1:
            fields[app] = new
            for side in range(2):
                where_inside(SIDES[side], halo_copy(app + 1, side, field(app + 1)).start)
        else:
            out_ref[0] = new

    for copy in sent:
        copy.wait_send()
    mate_copy().wait_send()
    for n in range(len(REACHED_BY_MATE)):
        where_inside(REACHED_BY_MATE[n], mate_part_copy(n).wait_send)
    for n in range(2):
        where_inside(SIDES[n], kb_copy(n).wait_send)
    for app in range(DEGREE):
        for side in range(2):
            where_inside(SIDES[side], halo_copy(app, side, field(app)).wait_send)
        for n in range(len(REACHED)):
            where_inside(REACHED[n], part_copy(app, n).wait_send)


def on_device(wave_block, potential, projectors, kb_energy, slot_atom, slot_corner):
    vmem, hbm = pl.BlockSpec(memory_space=pltpu.VMEM), pl.BlockSpec(memory_space=pltpu.HBM)
    dma = pltpu.SemaphoreType.DMA
    return pl.pallas_call(
        kernel,
        out_shape=jax.ShapeDtypeStruct(wave_block.shape, F32),
        in_specs=[hbm] * 6,
        out_specs=vmem,
        scratch_shapes=[
            pltpu.VMEM((CX, CY, CZ), F32),
            pltpu.VMEM((CX, CY, CZ), F32),
            pltpu.VMEM((SLOTS * PROJ, 128), F32),
            pltpu.VMEM((8, ATOM_DEV), F32),
            pltpu.SMEM((SLOTS,), jnp.int32),
            pltpu.SMEM((3, SLOTS), jnp.int32),
            dma((6,)),
            pltpu.VMEM((2 * SX, PROJ, 8, LANES), F32),
            pltpu.VMEM((DEGREE, 2, REACH, CY, CZ), F32),
            pltpu.VMEM((DEGREE, 8, 128), F32),
            pltpu.VMEM((DEGREE, len(REACHED), 8, 128), F32),
            pltpu.VMEM((8, 128), F32),
            pltpu.VMEM((2, 8, 128), F32),
            pltpu.VMEM((DEGREE - 1, CX, CY, CZ), F32),
            pltpu.VMEM((2 * SX, 8, LANES), F32),
            pltpu.VMEM((PROJ, 8, LANES), F32),
            pltpu.VMEM((ROWS, LANES), F32),
            pltpu.VMEM((SX, CY, CZ), F32),
            pltpu.VMEM((SX, 8, LANES), F32),
            pltpu.VMEM((PROJ, 8, LANES), F32),
            pltpu.VMEM((8, 128), F32),
            pltpu.VMEM((len(REACHED_BY_MATE), 8, 128), F32),
            pltpu.VMEM((CZ, LANES), BF16),
            pltpu.VMEM((LANES, CZ), BF16),
            pltpu.VMEM((128, LANES), BF16),
            pltpu.VMEM((LANES, 128), BF16),
            pltpu.VMEM((CZ, 256), BF16),
            pltpu.VMEM((2 * ROWS, ROWS), BF16),
            pltpu.VMEM((8, LANES), jnp.int32),
            pltpu.VMEM((CX, CY, CZ), F32),
            dma((3, SENDS)),
            dma((3, SENDS)),
            dma((1 + len(REACHED_BY_MATE),)),
            dma((1 + len(REACHED_BY_MATE),)),
            dma((DEGREE, 2)),
            dma((DEGREE, 2)),
            dma((DEGREE, len(REACHED))),
            dma((DEGREE, len(REACHED))),
            dma((2,)),
            dma((2,)),
        ],
        compiler_params=pltpu.CompilerParams(
            collective_id=0, has_side_effects=True, vmem_limit_bytes=60 * 1024 * 1024
        ),
        name="chebyshev",
    )(wave_block, potential, projectors.reshape(SLOTS * PROJ, 128), kb_energy.T, slot_atom, slot_corner)


def solution(mesh):
    placed = (
        P("band", "dom", None, None),
        P("dom", None, None),
        P("dom", None, "band"),
        P("dom", None),
        P("dom"),
        P(None, "dom"),
    )
    return jax.shard_map(
        on_device,
        mesh=mesh,
        in_specs=placed,
        out_specs=P("band", "dom", None, None),
        check_vma=False,
    )
```

```python
import functools

import jax
import jax.numpy as jnp
from jax import lax
from jax.experimental import pallas as pl
from jax.experimental.pallas import tpu as pltpu
from jax.sharding import PartitionSpec as P

SX, SY, SZ, DEGREE, PROJ = 8, 16, 16, 3, 8
CX, CY, CZ = 12, 16, 128
SLOTS, ATOM_DEV = 32, 16
LANES = SLOTS * SZ
ROWS = CX * CY
REACH = 6
Y_RING = 8
PARTS = 4
HALF = PARTS // 2
PROJ_PART = PROJ // PARTS
RING_PARTS = (2, 2, 2)
RING_SENDS = 3 * PARTS + HALF + sum(RING_PARTS)
Z_SENDS = 2 * PARTS + 2 * sum(PARTS - count for count in RING_PARTS)
SENDS = max(RING_SENDS, Z_SENDS)
STENCIL = (
    -5369.0 / 1800.0,
    12.0 / 7.0,
    -15.0 / 56.0,
    10.0 / 189.0,
    -1.0 / 112.0,
    2.0 / 1925.0,
    -1.0 / 16632.0,
)
KINETIC = tuple(-0.5 * weight for weight in STENCIL)
LOWER_EDGE, UPPER_EDGE, ANCHOR_POINT = 3.0, 30.0, 0.5
F32, BF16 = jnp.float32, jnp.bfloat16
MESH = pl.DeviceIdType.MESH
REACHED = (1, 2, -1, -2)
REACHED_BY_MATE = (0,) + REACHED
SIDES = (1, -1)


def split(x):
    high = x.astype(BF16)
    return high, (x - high.astype(F32)).astype(BF16)


def halves_beside(x):
    return jnp.concatenate(split(x), axis=1)


def dot_below(x, table):
    rows = x.shape[0]
    high = x.astype(BF16).astype(F32)
    both = dot(jnp.concatenate([high, x - high], axis=0).astype(BF16), table)
    return both[0:rows] + both[rows:]


def dot(a, b):
    return jnp.dot(a, b, preferred_element_type=F32)


def iota(shape, dim):
    return lax.broadcasted_iota(jnp.int32, shape, dim)


def weight_at(distance, centre):
    out = jnp.where(distance == 0, F32(centre), F32(0.0))
    for k in range(1, REACH + 1):
        out = jnp.where(distance == k, F32(KINETIC[k]), out)
    return out


def coefficients():
    half_width = (UPPER_EDGE - LOWER_EDGE) / 2.0
    centre = (UPPER_EDGE + LOWER_EDGE) / 2.0
    sigma_first = half_width / (ANCHOR_POINT - centre)
    out = [(sigma_first / half_width, 0.0)]
    sigma = sigma_first
    for _ in range(2, DEGREE + 1):
        following = 1.0 / (2.0 / sigma_first - sigma)
        out.append((2.0 * following / half_width, sigma * following))
        sigma = following
    return centre, out


def transposed_parts(x):
    row, col = iota((8, 128), 0), iota((8, 128), 1) >> 4
    for bit in (1, 2, 4):
        row_bit, col_bit = (row & bit) != 0, (col & bit) != 0
        down = pltpu.roll(pltpu.roll(x, bit, 0), 128 - 16 * bit, 1)
        up = pltpu.roll(pltpu.roll(x, 8 - bit, 0), 16 * bit, 1)
        x = jnp.where(row_bit == col_bit, x, jnp.where(row_bit, down, up))
    return x


def kernel(
    wave_hbm, pot_hbm, proj_hbm, kb_hbm, atom_hbm, corner_hbm, out_ref,
    wave_ref, pot_ref, proj_ref, kb_fetched, atom_ref, corner_ref, fetched,
    pbuf, halo, part_own, part_in, kb_own, kb_in, fields, boxes, acc, deposit_in,
    mate_field, mate_boxes, mate_acc, mate_part, mate_part_in,
    pick_z, pick_zt, pick_atom, pick_atom_t, band_z, cross, x_corner, local,
    gather_out, gather_in, mate_out_sem, mate_in_sem, halo_out, halo_in_sem, part_out_sem, part_in_sem, kb_out_sem, kb_in_sem,
):
    dom, band = lax.axis_index("dom"), lax.axis_index("band")
    doms = lax.axis_size("dom")
    y, z = lax.rem(band, Y_RING), lax.div(band, Y_RING)

    def inside(step):
        return (dom + step >= 0) & (dom + step < doms)

    def where_inside(step, work):
        pl.when(inside(step))(work)

    def band_at(dy, other):
        column = 1 - z if other else z
        return column * Y_RING + lax.rem(y + dy + Y_RING, Y_RING)

    gather_to = (band_at(1, False), band_at(-1, False), band_at(0, True))

    barrier = pltpu.get_barrier_semaphore()
    for target in gather_to:
        pl.semaphore_signal(barrier, inc=1, device_id=(dom, target), device_id_type=MESH)
    for step in REACHED:

        @functools.partial(where_inside, step)
        def _():
            for target in (band, gather_to[2]):
                pl.semaphore_signal(barrier, inc=1, device_id=(dom + step, target), device_id_type=MESH)

    kb_own[...] = jnp.zeros((8, 128), F32)
    fetches = [
        pltpu.make_async_copy(source, target, fetched.at[n])
        for n, (source, target) in enumerate(
            (
                (proj_hbm, proj_ref),
                (wave_hbm.at[0], wave_ref),
                (corner_hbm, corner_ref),
                (atom_hbm, atom_ref),
                (kb_hbm, kb_fetched),
                (pot_hbm, pot_ref),
            )
        )
    ]
    for fetch in fetches:
        fetch.start()

    def piece(way, n, owner, part):
        ref = pbuf.at[owner, pl.ds(part * PROJ_PART, PROJ_PART)]
        return pltpu.make_async_remote_copy(
            src_ref=ref, dst_ref=ref, send_sem=gather_out.at[way, n], recv_sem=gather_in.at[way, n],
            device_id=(dom, gather_to[way]), device_id_type=MESH,
        )

    sent = []

    def send(way, n, owner, part):
        copy = piece(way, n, owner, part)
        copy.start()
        sent.append(copy)

    def received(way, n, owner, part):
        piece(way, n, owner, part).wait_recv()

    fetches[0].wait()
    for part in range(PARTS):
        for p in range(part * PROJ_PART, (part + 1) * PROJ_PART):
            for g in range(4):
                x = proj_ref[pl.ds(64 * g + p, 8, stride=8), :]
                pbuf[band, p, :, pl.ds(128 * g, 128)] = transposed_parts(x)
        if part == 0:
            pl.semaphore_wait(barrier, 3 + 2 * sum(inside(step).astype(jnp.int32) for step in REACHED))
        for way in range(3):
            send(way, part, band, part)

    def halo_copy(app, side, source):
        planes = pl.ds(CX - REACH, REACH) if side == 0 else pl.ds(0, REACH)
        return pltpu.make_async_remote_copy(
            src_ref=source.at[planes], dst_ref=halo.at[app, side],
            send_sem=halo_out.at[app, side], recv_sem=halo_in_sem.at[app, side],
            device_id=(dom + (1 if side == 0 else -1), band), device_id_type=MESH,
        )

    def part_copy(app, n):
        return pltpu.make_async_remote_copy(
            src_ref=part_own.at[app], dst_ref=part_in.at[app, n],
            send_sem=part_out_sem.at[app, n], recv_sem=part_in_sem.at[app, n],
            device_id=(dom + REACHED[n], band), device_id_type=MESH,
        )

    def mate_copy():
        return pltpu.make_async_remote_copy(
            src_ref=wave_ref.at[pl.ds((SX // 2) * (1 - z), SX)], dst_ref=mate_field,
            send_sem=mate_out_sem.at[0], recv_sem=mate_in_sem.at[0],
            device_id=(dom, gather_to[2]), device_id_type=MESH,
        )

    def mate_part_copy(n):
        return pltpu.make_async_remote_copy(
            src_ref=mate_part, dst_ref=mate_part_in.at[n],
            send_sem=mate_out_sem.at[1 + n], recv_sem=mate_in_sem.at[1 + n],
            device_id=(dom + REACHED_BY_MATE[n], gather_to[2]), device_id_type=MESH,
        )

    def kb_copy(n):
        return pltpu.make_async_remote_copy(
            src_ref=kb_own, dst_ref=kb_in.at[n], send_sem=kb_out_sem.at[n], recv_sem=kb_in_sem.at[n],
            device_id=(dom + (1 if n == 0 else -1), band), device_id_type=MESH,
        )

    def field(app):
        return wave_ref if app == 0 else fields.at[app - 1]

    for fetch in fetches[1:]:
        fetch.wait()
    kb_own[:, 0:ATOM_DEV] = kb_fetched[...]
    mate_copy().start()
    for n in range(2):
        where_inside(SIDES[n], kb_copy(n).start)
    for side in range(2):
        where_inside(SIDES[side], halo_copy(0, side, field(0)).start)

    def make_picks():
        lane = iota((8, 128), 1)
        lane_slot, lane_cell = lane >> 4, lane & 15
        pad_rows = iota((128, 128), 0)
        first_atom = (dom - 1) * ATOM_DEV
        for g in range(4):
            at_x, at_z, atom = (jnp.zeros((8, 128), jnp.int32) for _ in range(3))
            for q in range(8):
                here = lane_slot == q
                at_x = jnp.where(here, corner_ref[0, 8 * g + q], at_x)
                at_z = jnp.where(here, corner_ref[2, 8 * g + q], at_z)
                atom = jnp.where(here, atom_ref[8 * g + q] - first_atom, atom)
            lanes = pl.ds(128 * g, 128)
            x_corner[:, lanes] = at_x
            hot_z = jnp.where(pad_rows == (at_z + lane_cell)[0:1, :], F32(1.0), F32(0.0))
            pick_z[0:CZ, lanes] = pick_z[CZ:, lanes] = hot_z.astype(BF16)
            pick_zt[lanes, :] = jnp.transpose(hot_z).astype(BF16)
            hot_atom = jnp.where(pad_rows == atom[0:1, :], F32(1.0), F32(0.0))
            pick_atom[:, lanes] = hot_atom.astype(BF16)
            pick_atom_t[lanes, :] = jnp.transpose(hot_atom).astype(BF16)

    def extract(planes, out):
        count = out.shape[0] // 2
        extent = count + CX - SX
        rows = halves_beside(planes[...].reshape(extent * CY, CZ))
        for g in range(4):
            lanes = pl.ds(128 * g, 128)
            along_z = dot(rows, pick_z[:, lanes]).reshape(extent, CY, 128)
            at_x = x_corner[:, lanes][None, 0:1, :]
            cut = along_z[0:count]
            for d in range(1, CX - SX + 1):
                cut = jnp.where(at_x == d, along_z[d : d + count], cut)
            out[:, :, lanes] = cut.reshape(2 * count, 8, 128)

    def make_stencil():
        distance = jnp.abs(iota((CZ, CZ), 0) - iota((CZ, CZ), 1))
        band_z[:, 0:128], band_z[:, 128:256] = split(weight_at(distance, 3.0 * KINETIC[0]))
        row, col = iota((ROWS, ROWS), 0), iota((ROWS, ROWS), 1)
        gap_x, gap_y = jnp.abs((row >> 4) - (col >> 4)), jnp.abs((row & 15) - (col & 15))
        gap = jnp.where(gap_x == 0, gap_y, jnp.where(gap_y == 0, gap_x, 99))
        cross[0:ROWS, :], cross[ROWS:, :] = split(weight_at(gap, 0.0))

    def accumulate(step, part, own=True, mate=True):
        owner, at = band_at(step, False), lax.rem(y + step + Y_RING, Y_RING)
        here = pl.ds(part * PROJ_PART, PROJ_PART)
        values = pbuf[owner, here]
        for wanted, total, cells in ((own, acc, boxes[owner]), (mate, mate_acc, mate_boxes[at])):
            if wanted:
                term = values * cells[None]
                total[here] = term if step == 0 else total[here] + term

    def atom_partials(total):
        by_slot = jnp.sum(total[...], axis=1)
        return dot_below(by_slot, pick_atom_t[...])

    def apply_local(app):
        rows = field(app)[...].reshape(ROWS, CZ)
        high, low = split(rows)
        weights = band_z[...]
        both = dot(high, weights)
        out = both[:, 0:128] + both[:, 128:256] + dot(low, weights[:, 0:128])
        both = dot(cross[...], jnp.concatenate([high, low], axis=1))
        out = out + (both[0:ROWS, 0:128] + both[0:ROWS, 128:256] + both[ROWS:, 0:128])
        out = out + pot_ref[...].reshape(ROWS, CZ) * rows
        local[...] = out.reshape(CX, CY, CZ)

    def add_halo(app):
        for side in range(2):
            where_inside(-SIDES[side], halo_copy(app, side, field(app)).wait_recv)
        low = jnp.where(dom > 0, halo[app, 0], F32(0.0))
        high = jnp.where(dom < doms - 1, halo[app, 1], F32(0.0))
        for x in range(REACH):
            local[x] = local[x] + sum(F32(KINETIC[k]) * low[REACH + x - k] for k in range(x + 1, REACH + 1))
            at = CX - 1 - x
            local[at] = local[at] + sum(F32(KINETIC[k]) * high[k - 1 - x] for k in range(x + 1, REACH + 1))

    all_parts = tuple(range(PARTS))
    halves = all_parts[:HALF], all_parts[HALF:]
    ways = ((0, -1), (1, 1))
    z_expected = [(band_at(0, True), part) for part in all_parts]
    z_waiting = []

    def to_mate(step, part):
        z_waiting.append((step, part))

    def flush_to_mate():
        for step, part in z_waiting:
            send(2, len(z_expected), band_at(step, False), part)
            z_expected.append((band_at(step, True), part))
        z_waiting.clear()

    def other_ring(hop, part):
        return 3 * PARTS + HALF + sum(RING_PARTS[: hop + 1]) + part - PARTS

    def pass_other(hop):
        for part in range(PARTS - RING_PARTS[max(hop - 1, 0)], PARTS):
            for way, sign in ways:
                owner = band_at(sign * hop, True)
                if hop:
                    received(way, other_ring(hop - 1, part), owner, part)
                elif way == 0:
                    received(2, part, owner, part)
                if hop < 3 and part >= PARTS - RING_PARTS[hop]:
                    send(way, other_ring(hop, part), owner, part)

    for step in range(1, 4):
        for part in all_parts:
            for way, sign in ways:
                owner = band_at(sign * step, False)
                received(way, (step - 1) * PARTS + part, owner, part)
                if step < 3:
                    send(way, step * PARTS + part, owner, part)
                elif part in halves[way]:
                    send(way, 3 * PARTS + part - halves[way][0], owner, part)
                if part < PARTS - RING_PARTS[step - 1]:
                    to_mate(sign * step, part)
                    flush_to_mate()
        pass_other(step - 1)
        if step == 1:
            make_picks()
            extract(field(0), boxes)
            for part in all_parts:
                accumulate(0, part, mate=False)
                for sign in (-1, 1):
                    accumulate(sign, part, mate=False)
        elif step == 2:
            mate_copy().wait_recv()
            extract(mate_field, mate_boxes)
            for part in all_parts:
                accumulate(0, part, own=False)
                for sign in (-1, 1):
                    accumulate(sign, part, own=False)
                    accumulate(2 * sign, part)
        else:
            for part in all_parts:
                for sign in (-1, 1):
                    accumulate(3 * sign, part)
    for part in range(HALF):
        for way, sign in ways:
            at = halves[way][part]
            received(way, 3 * PARTS + part, band_at(4, False), at)
            to_mate(4, at)
            flush_to_mate()
            accumulate(4, at)
    part_own[0] = atom_partials(acc)
    mate_part[...] = atom_partials(mate_acc)
    for n in range(len(REACHED)):
        where_inside(REACHED[n], part_copy(0, n).start)
        where_inside(REACHED[n], mate_part_copy(n + 1).start)
    mate_part_copy(0).start()
    pass_other(3)
    make_stencil()
    apply_local(0)
    for n, (owner, part) in enumerate(z_expected):
        if n >= PARTS or part < PARTS - RING_PARTS[0]:
            received(2, n, owner, part)
    add_halo(0)

    for n in range(2):
        where_inside(-SIDES[n], kb_copy(n).wait_recv)
    atom_lane = iota((8, 128), 1)
    energy = jnp.where(
        atom_lane < ATOM_DEV,
        jnp.where(dom > 0, kb_in[0], F32(0.0)),
        jnp.where(
            atom_lane < 2 * ATOM_DEV,
            pltpu.roll(kb_own[...], ATOM_DEV, 1),
            jnp.where((atom_lane < 3 * ATOM_DEV) & (dom < doms - 1), pltpu.roll(kb_in[1], 2 * ATOM_DEV, 1), F32(0.0)),
        ),
    )
    centre, coefs = coefficients()
    for app in range(DEGREE):
        if app:
            extract(field(app), boxes)
            for g in range(4):
                lanes = pl.ds(128 * g, 128)
                total = pbuf[0, :, :, lanes] * boxes[0, :, lanes][None]
                for owner in range(1, 2 * SX):
                    total = total + pbuf[owner, :, :, lanes] * boxes[owner, :, lanes][None]
                acc[:, :, lanes] = total
            part_own[app] = atom_partials(acc)
            for n in range(len(REACHED)):
                where_inside(REACHED[n], part_copy(app, n).start)
            apply_local(app)
            add_halo(app)
        total = part_own[app]
        if app == 0:
            mate_part_copy(0).wait_recv()
            total = total + mate_part_in[0]
        for n, step in enumerate(REACHED):
            where_inside(-step, part_copy(app, n).wait_recv)
            partial = part_in[app, n]
            if app == 0:
                where_inside(-step, mate_part_copy(n + 1).wait_recv)
                partial = partial + mate_part_in[n + 1]
            shifted = pltpu.roll(partial, (-step * ATOM_DEV) % 128, 1)
            total = total + jnp.where(inside(-step), shifted, F32(0.0))
        back_all = dot_below(total * energy, pick_atom[...])
        for g in range(4):
            lanes = pl.ds(128 * g, 128)
            back = back_all[:, 128 * g : 128 * (g + 1)]
            weights = [jnp.broadcast_to(back[p : p + 1, :], (8, 128)) for p in range(PROJ)]
            at_x = x_corner[:, lanes]
            for half in range(2):
                values = []
                for i in range(SX):
                    value = pbuf[2 * i + half, 0, :, lanes] * weights[0]
                    for p in range(1, PROJ):
                        value = value + pbuf[2 * i + half, p, :, lanes] * weights[p]
                    values.append(value)
                for x in range(CX):
                    spread = jnp.zeros((8, 128), F32)
                    for d in range(max(0, x - SX + 1), min(x, CX - SX) + 1):
                        spread = jnp.where(at_x == d, values[x - d], spread)
                    deposit_in[pl.ds(x * CY + 8 * half, 8), lanes] = spread
        nonlocal_part = dot_below(deposit_in[...], pick_zt[...]).reshape(CX, CY, CZ)
        now = field(app)[...]
        scale, keep = coefs[app]
        new = F32(scale) * (local[...] + nonlocal_part - F32(centre) * now)
        if app:
            new = new - F32(keep) * field(app - 1)[...]
        if app < DEGREE - 1:
            fields[app] = new
            for side in range(2):
                where_inside(SIDES[side], halo_copy(app + 1, side, field(app + 1)).start)
        else:
            out_ref[0] = new

    for copy in sent:
        copy.wait_send()
    mate_copy().wait_send()
    for n in range(len(REACHED_BY_MATE)):
        where_inside(REACHED_BY_MATE[n], mate_part_copy(n).wait_send)
    for n in range(2):
        where_inside(SIDES[n], kb_copy(n).wait_send)
    for app in range(DEGREE):
        for side in range(2):
            where_inside(SIDES[side], halo_copy(app, side, field(app)).wait_send)
        for n in range(len(REACHED)):
            where_inside(REACHED[n], part_copy(app, n).wait_send)


def on_device(wave_block, potential, projectors, kb_energy, slot_atom, slot_corner):
    vmem, hbm = pl.BlockSpec(memory_space=pltpu.VMEM), pl.BlockSpec(memory_space=pltpu.HBM)
    dma = pltpu.SemaphoreType.DMA
    return pl.pallas_call(
        kernel,
        out_shape=jax.ShapeDtypeStruct(wave_block.shape, F32),
        in_specs=[hbm] * 6,
        out_specs=vmem,
        scratch_shapes=[
            pltpu.VMEM((CX, CY, CZ), F32),
            pltpu.VMEM((CX, CY, CZ), F32),
            pltpu.VMEM((SLOTS * PROJ, 128), F32),
            pltpu.VMEM((8, ATOM_DEV), F32),
            pltpu.SMEM((SLOTS,), jnp.int32),
            pltpu.SMEM((3, SLOTS), jnp.int32),
            dma((6,)),
            pltpu.VMEM((2 * SX, PROJ, 8, LANES), F32),
            pltpu.VMEM((DEGREE, 2, REACH, CY, CZ), F32),
            pltpu.VMEM((DEGREE, 8, 128), F32),
            pltpu.VMEM((DEGREE, len(REACHED), 8, 128), F32),
            pltpu.VMEM((8, 128), F32),
            pltpu.VMEM((2, 8, 128), F32),
            pltpu.VMEM((DEGREE - 1, CX, CY, CZ), F32),
            pltpu.VMEM((2 * SX, 8, LANES), F32),
            pltpu.VMEM((PROJ, 8, LANES), F32),
            pltpu.VMEM((ROWS, LANES), F32),
            pltpu.VMEM((SX, CY, CZ), F32),
            pltpu.VMEM((SX, 8, LANES), F32),
            pltpu.VMEM((PROJ, 8, LANES), F32),
            pltpu.VMEM((8, 128), F32),
            pltpu.VMEM((len(REACHED_BY_MATE), 8, 128), F32),
            pltpu.VMEM((2 * CZ, LANES), BF16),
            pltpu.VMEM((LANES, CZ), BF16),
            pltpu.VMEM((128, LANES), BF16),
            pltpu.VMEM((LANES, 128), BF16),
            pltpu.VMEM((CZ, 256), BF16),
            pltpu.VMEM((2 * ROWS, ROWS), BF16),
            pltpu.VMEM((8, LANES), jnp.int32),
            pltpu.VMEM((CX, CY, CZ), F32),
            dma((3, SENDS)),
            dma((3, SENDS)),
            dma((1 + len(REACHED_BY_MATE),)),
            dma((1 + len(REACHED_BY_MATE),)),
            dma((DEGREE, 2)),
            dma((DEGREE, 2)),
            dma((DEGREE, len(REACHED))),
            dma((DEGREE, len(REACHED))),
            dma((2,)),
            dma((2,)),
        ],
        compiler_params=pltpu.CompilerParams(
            collective_id=0, has_side_effects=True, vmem_limit_bytes=56 * 1024 * 1024
        ),
        name="chebyshev",
    )(wave_block, potential, projectors.reshape(SLOTS * PROJ, 128), kb_energy.T, slot_atom, slot_corner)


def solution(mesh):
    placed = (
        P("band", "dom", None, None),
        P("dom", None, None),
        P("dom", None, "band"),
        P("dom", None),
        P("dom"),
        P(None, "dom"),
    )
    return jax.shard_map(
        on_device,
        mesh=mesh,
        in_specs=placed,
        out_specs=P("band", "dom", None, None),
        check_vma=False,
    )
```

```python
import functools

import jax
import jax.numpy as jnp
from jax import lax
from jax.experimental import pallas as pl
from jax.experimental.pallas import tpu as pltpu
from jax.sharding import PartitionSpec as P

SX, SY, SZ, DEGREE, PROJ = 8, 16, 16, 3, 8
CX, CY, CZ = 12, 16, 128
SLOTS, ATOM_DEV = 32, 16
LANES = SLOTS * SZ
ROWS = CX * CY
REACH = 6
Y_RING = 8
PARTS = 4
HALF = PARTS // 2
PROJ_PART = PROJ // PARTS
RING_PARTS = (2, 2, 2)
RING_SENDS = 3 * PARTS + HALF + sum(RING_PARTS)
Z_SENDS = 2 * PARTS + 2 * sum(PARTS - count for count in RING_PARTS)
SENDS = max(RING_SENDS, Z_SENDS)
STENCIL = (
    -5369.0 / 1800.0,
    12.0 / 7.0,
    -15.0 / 56.0,
    10.0 / 189.0,
    -1.0 / 112.0,
    2.0 / 1925.0,
    -1.0 / 16632.0,
)
KINETIC = tuple(-0.5 * weight for weight in STENCIL)
LOWER_EDGE, UPPER_EDGE, ANCHOR_POINT = 3.0, 30.0, 0.5
F32, BF16 = jnp.float32, jnp.bfloat16
MESH = pl.DeviceIdType.MESH
REACHED = (1, 2, -1, -2)
REACHED_BY_MATE = (0,) + REACHED
SIDES = (1, -1)


def split(x):
    high = x.astype(BF16)
    return high, (x - high.astype(F32)).astype(BF16)


def halves_beside(x):
    return jnp.concatenate(split(x), axis=1)


def dot_below(x, table):
    rows = x.shape[0]
    high = x.astype(BF16).astype(F32)
    both = dot(jnp.concatenate([high, x - high], axis=0).astype(BF16), table)
    return both[0:rows] + both[rows:]


def dot(a, b):
    return jnp.dot(a, b, preferred_element_type=F32)


def iota(shape, dim):
    return lax.broadcasted_iota(jnp.int32, shape, dim)


def weight_at(distance, centre):
    out = jnp.where(distance == 0, F32(centre), F32(0.0))
    for k in range(1, REACH + 1):
        out = jnp.where(distance == k, F32(KINETIC[k]), out)
    return out


def coefficients():
    half_width = (UPPER_EDGE - LOWER_EDGE) / 2.0
    centre = (UPPER_EDGE + LOWER_EDGE) / 2.0
    sigma_first = half_width / (ANCHOR_POINT - centre)
    out = [(sigma_first / half_width, 0.0)]
    sigma = sigma_first
    for _ in range(2, DEGREE + 1):
        following = 1.0 / (2.0 / sigma_first - sigma)
        out.append((2.0 * following / half_width, sigma * following))
        sigma = following
    return centre, out


def transposed_parts(x):
    row, col = iota((8, 128), 0), iota((8, 128), 1) >> 4
    for bit in (1, 2, 4):
        row_bit, col_bit = (row & bit) != 0, (col & bit) != 0
        down = pltpu.roll(pltpu.roll(x, bit, 0), 128 - 16 * bit, 1)
        up = pltpu.roll(pltpu.roll(x, 8 - bit, 0), 16 * bit, 1)
        x = jnp.where(row_bit == col_bit, x, jnp.where(row_bit, down, up))
    return x


def kernel(
    wave_hbm, pot_hbm, proj_hbm, kb_hbm, atom_hbm, corner_hbm, out_ref,
    wave_ref, pot_ref, proj_ref, kb_fetched, atom_ref, corner_ref, fetched,
    pbuf, halo, part_own, part_in, kb_own, kb_in, fields, boxes, acc, deposit_in,
    mate_field, mate_boxes, mate_acc, mate_part, mate_part_in,
    pick_z, pick_zt, pick_atom, pick_atom_t, band_z, cross, x_corner, local,
    gather_out, gather_in, mate_out_sem, mate_in_sem, halo_out, halo_in_sem, part_out_sem, part_in_sem, kb_out_sem, kb_in_sem,
):
    dom, band = lax.axis_index("dom"), lax.axis_index("band")
    doms = lax.axis_size("dom")
    y, z = lax.rem(band, Y_RING), lax.div(band, Y_RING)

    def inside(step):
        return (dom + step >= 0) & (dom + step < doms)

    def where_inside(step, work):
        pl.when(inside(step))(work)

    def band_at(dy, other):
        column = 1 - z if other else z
        return column * Y_RING + lax.rem(y + dy + Y_RING, Y_RING)

    gather_to = (band_at(1, False), band_at(-1, False), band_at(0, True))

    barrier = pltpu.get_barrier_semaphore()
    for target in gather_to:
        pl.semaphore_signal(barrier, inc=1, device_id=(dom, target), device_id_type=MESH)
    for step in REACHED:

        @functools.partial(where_inside, step)
        def _():
            for target in (band, gather_to[2]):
                pl.semaphore_signal(barrier, inc=1, device_id=(dom + step, target), device_id_type=MESH)

    kb_own[...] = jnp.zeros((8, 128), F32)
    fetches = [
        pltpu.make_async_copy(source, target, fetched.at[n])
        for n, (source, target) in enumerate(
            (
                (proj_hbm, proj_ref.at[pl.ds(0, SLOTS * PROJ)]),
                (wave_hbm.at[0], wave_ref),
                (corner_hbm, corner_ref),
                (atom_hbm, atom_ref),
                (kb_hbm, kb_fetched),
                (pot_hbm, pot_ref),
            )
        )
    ]
    for fetch in fetches:
        fetch.start()

    def piece(way, n, owner, part):
        ref = pbuf.at[owner, pl.ds(part * PROJ_PART, PROJ_PART)]
        return pltpu.make_async_remote_copy(
            src_ref=ref, dst_ref=ref, send_sem=gather_out.at[way, n], recv_sem=gather_in.at[way, n],
            device_id=(dom, gather_to[way]), device_id_type=MESH,
        )

    sent = []

    def send(way, n, owner, part):
        copy = piece(way, n, owner, part)
        copy.start()
        sent.append(copy)

    def received(way, n, owner, part):
        piece(way, n, owner, part).wait_recv()

    fetches[0].wait()
    for part in range(PARTS):
        for p in range(part * PROJ_PART, (part + 1) * PROJ_PART):
            for g in range(4):
                x = proj_ref[pl.ds(64 * g + p, 8, stride=8), :]
                pbuf[band, p, :, pl.ds(128 * g, 128)] = transposed_parts(x)
        if part == 0:
            pl.semaphore_wait(barrier, 3 + 2 * sum(inside(step).astype(jnp.int32) for step in REACHED))
        for way in (2, 0, 1):
            send(way, part, band, part)

    def halo_copy(app, side, source):
        planes = pl.ds(CX - REACH, REACH) if side == 0 else pl.ds(0, REACH)
        return pltpu.make_async_remote_copy(
            src_ref=source.at[planes], dst_ref=halo.at[app, side],
            send_sem=halo_out.at[app, side], recv_sem=halo_in_sem.at[app, side],
            device_id=(dom + (1 if side == 0 else -1), band), device_id_type=MESH,
        )

    def part_copy(app, n):
        return pltpu.make_async_remote_copy(
            src_ref=part_own.at[app], dst_ref=part_in.at[app, n],
            send_sem=part_out_sem.at[app, n], recv_sem=part_in_sem.at[app, n],
            device_id=(dom + REACHED[n], band), device_id_type=MESH,
        )

    def mate_copy():
        return pltpu.make_async_remote_copy(
            src_ref=wave_ref.at[pl.ds((SX // 2) * (1 - z), SX)], dst_ref=mate_field,
            send_sem=mate_out_sem.at[0], recv_sem=mate_in_sem.at[0],
            device_id=(dom, gather_to[2]), device_id_type=MESH,
        )

    def mate_part_copy(n):
        return pltpu.make_async_remote_copy(
            src_ref=mate_part, dst_ref=mate_part_in.at[n],
            send_sem=mate_out_sem.at[1 + n], recv_sem=mate_in_sem.at[1 + n],
            device_id=(dom + REACHED_BY_MATE[n], gather_to[2]), device_id_type=MESH,
        )

    def kb_copy(n):
        return pltpu.make_async_remote_copy(
            src_ref=kb_own, dst_ref=kb_in.at[n], send_sem=kb_out_sem.at[n], recv_sem=kb_in_sem.at[n],
            device_id=(dom + (1 if n == 0 else -1), band), device_id_type=MESH,
        )

    def field(app):
        return wave_ref if app == 0 else fields.at[app - 1]

    for fetch in fetches[1:]:
        fetch.wait()
    kb_own[:, 0:ATOM_DEV] = kb_fetched[...]
    mate_copy().start()
    for n in range(2):
        where_inside(SIDES[n], kb_copy(n).start)
    for side in range(2):
        where_inside(SIDES[side], halo_copy(0, side, field(0)).start)

    def make_picks():
        lane = iota((8, 128), 1)
        lane_slot, lane_cell = lane >> 4, lane & 15
        pad_rows = iota((128, 128), 0)
        first_atom = (dom - 1) * ATOM_DEV
        for g in range(4):
            at_x, at_z, atom = (jnp.zeros((8, 128), jnp.int32) for _ in range(3))
            for q in range(8):
                here = lane_slot == q
                at_x = jnp.where(here, corner_ref[0, 8 * g + q], at_x)
                at_z = jnp.where(here, corner_ref[2, 8 * g + q], at_z)
                atom = jnp.where(here, atom_ref[8 * g + q] - first_atom, atom)
            lanes = pl.ds(128 * g, 128)
            x_corner[:, lanes] = at_x
            hot_z = jnp.where(pad_rows == (at_z + lane_cell)[0:1, :], F32(1.0), F32(0.0))
            pick_z[0:CZ, lanes] = pick_z[CZ:, lanes] = hot_z.astype(BF16)
            pick_zt[lanes, :] = jnp.transpose(hot_z).astype(BF16)
            hot_atom = jnp.where(pad_rows == atom[0:1, :], F32(1.0), F32(0.0))
            pick_atom[:, lanes] = hot_atom.astype(BF16)
            pick_atom_t[lanes, :] = jnp.transpose(hot_atom).astype(BF16)

    def extract(planes, out):
        count = out.shape[0] // 2
        extent = count + CX - SX
        rows = halves_beside(planes[...].reshape(extent * CY, CZ))
        for g in range(4):
            lanes = pl.ds(128 * g, 128)
            along_z = dot(rows, pick_z[:, lanes]).reshape(extent, CY, 128)
            at_x = x_corner[:, lanes][None, 0:1, :]
            cut = along_z[0:count]
            for d in range(1, CX - SX + 1):
                cut = jnp.where(at_x == d, along_z[d : d + count], cut)
            out[:, :, lanes] = cut.reshape(2 * count, 8, 128)

    def make_stencil():
        distance = jnp.abs(iota((CZ, CZ), 0) - iota((CZ, CZ), 1))
        band_z[:, 0:128], band_z[:, 128:256] = split(weight_at(distance, 3.0 * KINETIC[0]))
        row, col = iota((ROWS, ROWS), 0), iota((ROWS, ROWS), 1)
        gap_x, gap_y = jnp.abs((row >> 4) - (col >> 4)), jnp.abs((row & 15) - (col & 15))
        gap = jnp.where(gap_x == 0, gap_y, jnp.where(gap_y == 0, gap_x, 99))
        cross[0:ROWS, :], cross[ROWS:, :] = split(weight_at(gap, 0.0))

    def accumulate(step, part, own=True, mate=True):
        owner, at = band_at(step, False), lax.rem(y + step + Y_RING, Y_RING)
        here = pl.ds(part * PROJ_PART, PROJ_PART)
        values = pbuf[owner, here]
        for wanted, total, cells in ((own, acc, boxes[owner]), (mate, mate_acc, mate_boxes[at])):
            if wanted:
                term = values * cells[None]
                total[here] = term if step == 0 else total[here] + term

    def atom_partials(total):
        by_slot = jnp.sum(total[...], axis=1)
        return dot_below(by_slot, pick_atom_t[...])

    def apply_local(app):
        rows = field(app)[...].reshape(ROWS, CZ)
        high, low = split(rows)
        weights = band_z[...]
        both = dot(high, weights)
        out = both[:, 0:128] + both[:, 128:256] + dot(low, weights[:, 0:128])
        both = dot(cross[...], jnp.concatenate([high, low], axis=1))
        out = out + (both[0:ROWS, 0:128] + both[0:ROWS, 128:256] + both[ROWS:, 0:128])
        out = out + pot_ref[...].reshape(ROWS, CZ) * rows
        local[...] = out.reshape(CX, CY, CZ)

    def add_halo(app):
        for side in range(2):
            where_inside(-SIDES[side], halo_copy(app, side, field(app)).wait_recv)
        low = jnp.where(dom > 0, halo[app, 0], F32(0.0))
        high = jnp.where(dom < doms - 1, halo[app, 1], F32(0.0))
        for x in range(REACH):
            local[x] = local[x] + sum(F32(KINETIC[k]) * low[REACH + x - k] for k in range(x + 1, REACH + 1))
            at = CX - 1 - x
            local[at] = local[at] + sum(F32(KINETIC[k]) * high[k - 1 - x] for k in range(x + 1, REACH + 1))

    all_parts = tuple(range(PARTS))
    halves = all_parts[:HALF], all_parts[HALF:]
    ways = ((0, -1), (1, 1))
    z_expected = [(band_at(0, True), part) for part in all_parts]
    z_waiting = []

    def to_mate(step, part):
        z_waiting.append((step, part))

    def flush_to_mate():
        for step, part in z_waiting:
            send(2, len(z_expected), band_at(step, False), part)
            z_expected.append((band_at(step, True), part))
        z_waiting.clear()

    def other_ring(hop, part):
        return 3 * PARTS + HALF + sum(RING_PARTS[: hop + 1]) + part - PARTS

    def pass_other(hop):
        for part in range(PARTS - RING_PARTS[max(hop - 1, 0)], PARTS):
            for way, sign in ways:
                owner = band_at(sign * hop, True)
                if hop:
                    received(way, other_ring(hop - 1, part), owner, part)
                elif way == 0:
                    received(2, part, owner, part)
                if hop < 3 and part >= PARTS - RING_PARTS[hop]:
                    send(way, other_ring(hop, part), owner, part)

    for step in range(1, 4):
        for part in all_parts:
            for way, sign in ways:
                owner = band_at(sign * step, False)
                received(way, (step - 1) * PARTS + part, owner, part)
                if step < 3:
                    send(way, step * PARTS + part, owner, part)
                elif part in halves[way]:
                    send(way, 3 * PARTS + part - halves[way][0], owner, part)
                if part < PARTS - RING_PARTS[step - 1]:
                    to_mate(sign * step, part)
                    flush_to_mate()
        pass_other(step - 1)
        if step == 1:
            make_picks()
            extract(field(0), boxes)
            for part in all_parts:
                accumulate(0, part, mate=False)
                for sign in (-1, 1):
                    accumulate(sign, part, mate=False)
        elif step == 2:
            mate_copy().wait_recv()
            extract(mate_field, mate_boxes)
            for part in all_parts:
                accumulate(0, part, own=False)
                for sign in (-1, 1):
                    accumulate(sign, part, own=False)
                    accumulate(2 * sign, part)
        else:
            for part in all_parts:
                for sign in (-1, 1):
                    accumulate(3 * sign, part)
    for part in range(HALF):
        for way, sign in ways:
            at = halves[way][part]
            received(way, 3 * PARTS + part, band_at(4, False), at)
            to_mate(4, at)
            flush_to_mate()
            accumulate(4, at)
    mate_part[...] = atom_partials(mate_acc)
    for n in range(len(REACHED)):
        where_inside(REACHED[n], mate_part_copy(n + 1).start)
    mate_part_copy(0).start()
    part_own[0] = atom_partials(acc)
    for n in range(len(REACHED)):
        where_inside(REACHED[n], part_copy(0, n).start)
    pass_other(3)
    make_stencil()
    apply_local(0)
    for n, (owner, part) in enumerate(z_expected):
        if n >= PARTS or part < PARTS - RING_PARTS[0]:
            received(2, n, owner, part)
    add_halo(0)

    for n in range(2):
        where_inside(-SIDES[n], kb_copy(n).wait_recv)
    atom_lane = iota((8, 128), 1)
    energy = jnp.where(
        atom_lane < ATOM_DEV,
        jnp.where(dom > 0, kb_in[0], F32(0.0)),
        jnp.where(
            atom_lane < 2 * ATOM_DEV,
            pltpu.roll(kb_own[...], ATOM_DEV, 1),
            jnp.where((atom_lane < 3 * ATOM_DEV) & (dom < doms - 1), pltpu.roll(kb_in[1], 2 * ATOM_DEV, 1), F32(0.0)),
        ),
    )
    def all_left(app):
        if app == 0:
            for copy in sent:
                copy.wait_send()
            mate_copy().wait_send()
            for n in range(len(REACHED_BY_MATE)):
                where_inside(REACHED_BY_MATE[n], mate_part_copy(n).wait_send)
            for n in range(2):
                where_inside(SIDES[n], kb_copy(n).wait_send)
        for side in range(2):
            where_inside(SIDES[side], halo_copy(app, side, field(app)).wait_send)
        for n in range(len(REACHED)):
            where_inside(REACHED[n], part_copy(app, n).wait_send)

    centre, coefs = coefficients()
    for app in range(DEGREE):
        if app:
            extract(field(app), boxes)
            for g in range(4):
                lanes = pl.ds(128 * g, 128)
                total = pbuf[0, :, :, lanes] * boxes[0, :, lanes][None]
                for owner in range(1, 2 * SX):
                    total = total + pbuf[owner, :, :, lanes] * boxes[owner, :, lanes][None]
                acc[:, :, lanes] = total
            part_own[app] = atom_partials(acc)
            for n in range(len(REACHED)):
                where_inside(REACHED[n], part_copy(app, n).start)
            apply_local(app)
            all_left(app - 1)
            add_halo(app)
        total = part_own[app]
        if app == 0:
            mate_part_copy(0).wait_recv()
            total = total + mate_part_in[0]
        for n, step in enumerate(REACHED):
            where_inside(-step, part_copy(app, n).wait_recv)
            partial = part_in[app, n]
            if app == 0:
                where_inside(-step, mate_part_copy(n + 1).wait_recv)
                partial = partial + mate_part_in[n + 1]
            shifted = pltpu.roll(partial, (-step * ATOM_DEV) % 128, 1)
            total = total + jnp.where(inside(-step), shifted, F32(0.0))
        back_all = dot_below(total * energy, pick_atom[...])
        for g in range(4):
            lanes = pl.ds(128 * g, 128)
            back = back_all[:, 128 * g : 128 * (g + 1)]
            weights = [jnp.broadcast_to(back[p : p + 1, :], (8, 128)) for p in range(PROJ)]
            at_x = x_corner[:, lanes]
            for half in range(2):
                values = []
                for i in range(SX):
                    value = pbuf[2 * i + half, 0, :, lanes] * weights[0]
                    for p in range(1, PROJ):
                        value = value + pbuf[2 * i + half, p, :, lanes] * weights[p]
                    values.append(value)
                for x in range(CX):
                    spread = jnp.zeros((8, 128), F32)
                    for d in range(max(0, x - SX + 1), min(x, CX - SX) + 1):
                        spread = jnp.where(at_x == d, values[x - d], spread)
                    deposit_in[pl.ds(x * CY + 8 * half, 8), lanes] = spread
        nonlocal_part = dot_below(deposit_in[...], pick_zt[...]).reshape(CX, CY, CZ)
        now = field(app)[...]
        scale, keep = coefs[app]
        new = F32(scale) * (local[...] + nonlocal_part - F32(centre) * now)
        if app:
            new = new - F32(keep) * field(app - 1)[...]
        if app < DEGREE - 1:
            fields[app] = new
            for side in range(2):
                where_inside(SIDES[side], halo_copy(app + 1, side, field(app + 1)).start)
        else:
            out_ref[0] = new

    all_left(DEGREE - 1)


def on_device(wave_block, potential, projectors, kb_energy, slot_atom, slot_corner):
    vmem, hbm = pl.BlockSpec(memory_space=pltpu.VMEM), pl.BlockSpec(memory_space=pltpu.HBM)
    dma = pltpu.SemaphoreType.DMA
    return pl.pallas_call(
        kernel,
        out_shape=jax.ShapeDtypeStruct(wave_block.shape, F32),
        in_specs=[hbm] * 6,
        out_specs=vmem,
        scratch_shapes=[
            pltpu.VMEM((CX, CY, CZ), F32),
            pltpu.VMEM((CX, CY, CZ), F32),
            pltpu.VMEM((SLOTS * PROJ + 8, 128), F32),
            pltpu.VMEM((8, ATOM_DEV), F32),
            pltpu.SMEM((SLOTS,), jnp.int32),
            pltpu.SMEM((3, SLOTS), jnp.int32),
            dma((6,)),
            pltpu.VMEM((2 * SX, PROJ, 8, LANES), F32),
            pltpu.VMEM((DEGREE, 2, REACH, CY, CZ), F32),
            pltpu.VMEM((DEGREE, 8, 128), F32),
            pltpu.VMEM((DEGREE, len(REACHED), 8, 128), F32),
            pltpu.VMEM((8, 128), F32),
            pltpu.VMEM((2, 8, 128), F32),
            pltpu.VMEM((DEGREE - 1, CX, CY, CZ), F32),
            pltpu.VMEM((2 * SX, 8, LANES), F32),
            pltpu.VMEM((PROJ, 8, LANES), F32),
            pltpu.VMEM((ROWS, LANES), F32),
            pltpu.VMEM((SX, CY, CZ), F32),
            pltpu.VMEM((SX, 8, LANES), F32),
            pltpu.VMEM((PROJ, 8, LANES), F32),
            pltpu.VMEM((8, 128), F32),
            pltpu.VMEM((len(REACHED_BY_MATE), 8, 128), F32),
            pltpu.VMEM((2 * CZ, LANES), BF16),
            pltpu.VMEM((LANES, CZ), BF16),
            pltpu.VMEM((128, LANES), BF16),
            pltpu.VMEM((LANES, 128), BF16),
            pltpu.VMEM((CZ, 256), BF16),
            pltpu.VMEM((2 * ROWS, ROWS), BF16),
            pltpu.VMEM((8, LANES), jnp.int32),
            pltpu.VMEM((CX, CY, CZ), F32),
            dma((3, SENDS)),
            dma((3, SENDS)),
            dma((1 + len(REACHED_BY_MATE),)),
            dma((1 + len(REACHED_BY_MATE),)),
            dma((DEGREE, 2)),
            dma((DEGREE, 2)),
            dma((DEGREE, len(REACHED))),
            dma((DEGREE, len(REACHED))),
            dma((2,)),
            dma((2,)),
        ],
        compiler_params=pltpu.CompilerParams(
            collective_id=0, has_side_effects=True, vmem_limit_bytes=56 * 1024 * 1024
        ),
        name="chebyshev",
    )(wave_block, potential, projectors.reshape(SLOTS * PROJ, 128), kb_energy.T, slot_atom, slot_corner)


def solution(mesh):
    placed = (
        P("band", "dom", None, None),
        P("dom", None, None),
        P("dom", None, "band"),
        P("dom", None),
        P("dom"),
        P(None, "dom"),
    )
    return jax.shard_map(
        on_device,
        mesh=mesh,
        in_specs=placed,
        out_specs=P("band", "dom", None, None),
        check_vma=False,
    )
```

```python
import functools

import jax
import jax.numpy as jnp
from jax import lax
from jax.experimental import pallas as pl
from jax.experimental.pallas import tpu as pltpu
from jax.sharding import PartitionSpec as P

SX, SY, SZ, DEGREE, PROJ = 8, 16, 16, 3, 8
CX, CY, CZ = 12, 16, 128
SLOTS, ATOM_DEV = 32, 16
LANES = SLOTS * SZ
ROWS = CX * CY
REACH = 6
Y_RING = 8
PARTS = 4
HALF = PARTS // 2
PROJ_PART = PROJ // PARTS
RING_PARTS = (2, 2, 2)
RING_SENDS = 3 * PARTS + HALF + sum(RING_PARTS)
Z_SENDS = 2 * PARTS + 2 * sum(PARTS - count for count in RING_PARTS)
SENDS = max(RING_SENDS, Z_SENDS)
STENCIL = (
    -5369.0 / 1800.0,
    12.0 / 7.0,
    -15.0 / 56.0,
    10.0 / 189.0,
    -1.0 / 112.0,
    2.0 / 1925.0,
    -1.0 / 16632.0,
)
KINETIC = tuple(-0.5 * weight for weight in STENCIL)
LOWER_EDGE, UPPER_EDGE, ANCHOR_POINT = 3.0, 30.0, 0.5
F32, BF16 = jnp.float32, jnp.bfloat16
MESH = pl.DeviceIdType.MESH
REACHED = (1, 2, -1, -2)
REACHED_BY_MATE = (0,) + REACHED
SIDES = (1, -1)


def split(x):
    high = x.astype(BF16)
    return high, (x - high.astype(F32)).astype(BF16)


def halves_beside(x):
    return jnp.concatenate(split(x), axis=1)


def dot_below(x, table):
    rows = x.shape[0]
    high = x.astype(BF16).astype(F32)
    both = dot(jnp.concatenate([high, x - high], axis=0).astype(BF16), table)
    return both[0:rows] + both[rows:]


def dot(a, b):
    return jnp.dot(a, b, preferred_element_type=F32)


def iota(shape, dim):
    return lax.broadcasted_iota(jnp.int32, shape, dim)


def weight_at(distance, centre):
    out = jnp.where(distance == 0, F32(centre), F32(0.0))
    for k in range(1, REACH + 1):
        out = jnp.where(distance == k, F32(KINETIC[k]), out)
    return out


def coefficients():
    half_width = (UPPER_EDGE - LOWER_EDGE) / 2.0
    centre = (UPPER_EDGE + LOWER_EDGE) / 2.0
    sigma_first = half_width / (ANCHOR_POINT - centre)
    out = [(sigma_first / half_width, 0.0)]
    sigma = sigma_first
    for _ in range(2, DEGREE + 1):
        following = 1.0 / (2.0 / sigma_first - sigma)
        out.append((2.0 * following / half_width, sigma * following))
        sigma = following
    return centre, out


def transposed_parts(x):
    row, col = iota((8, 128), 0), iota((8, 128), 1) >> 4
    for bit in (1, 2, 4):
        row_bit, col_bit = (row & bit) != 0, (col & bit) != 0
        down = pltpu.roll(pltpu.roll(x, bit, 0), 128 - 16 * bit, 1)
        up = pltpu.roll(pltpu.roll(x, 8 - bit, 0), 16 * bit, 1)
        x = jnp.where(row_bit == col_bit, x, jnp.where(row_bit, down, up))
    return x


def kernel(
    wave_hbm, pot_hbm, proj_hbm, kb_hbm, atom_hbm, corner_hbm, out_ref,
    wave_ref, pot_ref, proj_ref, kb_fetched, atom_ref, corner_ref, fetched,
    pbuf, halo, part_own, part_in, kb_own, kb_in, fields, boxes, acc, deposit_in,
    mate_field, mate_boxes, mate_acc, mate_part, mate_part_in,
    pick_z, pick_zt, pick_atom, pick_atom_t, band_z, cross, x_corner, local,
    gather_out, gather_in, mate_out_sem, mate_in_sem, halo_out, halo_in_sem, part_out_sem, part_in_sem, kb_out_sem, kb_in_sem,
):
    dom, band = lax.axis_index("dom"), lax.axis_index("band")
    doms = lax.axis_size("dom")
    y, z = lax.rem(band, Y_RING), lax.div(band, Y_RING)

    def inside(step):
        return (dom + step >= 0) & (dom + step < doms)

    def where_inside(step, work):
        pl.when(inside(step))(work)

    def band_at(dy, other):
        column = 1 - z if other else z
        return column * Y_RING + lax.rem(y + dy + Y_RING, Y_RING)

    gather_to = (band_at(1, False), band_at(-1, False), band_at(0, True))

    barrier = pltpu.get_barrier_semaphore()
    for target in gather_to:
        pl.semaphore_signal(barrier, inc=1, device_id=(dom, target), device_id_type=MESH)
    for step in REACHED:

        @functools.partial(where_inside, step)
        def _():
            for target in (band, gather_to[2]):
                pl.semaphore_signal(barrier, inc=1, device_id=(dom + step, target), device_id_type=MESH)

    kb_own[...] = jnp.zeros((8, 128), F32)
    fetches = [
        pltpu.make_async_copy(source, target, fetched.at[n])
        for n, (source, target) in enumerate(
            (
                (proj_hbm, proj_ref.at[pl.ds(0, SLOTS * PROJ)]),
                (wave_hbm.at[0], wave_ref),
                (corner_hbm, corner_ref),
                (atom_hbm, atom_ref),
                (kb_hbm, kb_fetched),
                (pot_hbm, pot_ref),
            )
        )
    ]
    for fetch in fetches:
        fetch.start()

    def piece(way, n, owner, part):
        ref = pbuf.at[owner, pl.ds(part * PROJ_PART, PROJ_PART)]
        return pltpu.make_async_remote_copy(
            src_ref=ref, dst_ref=ref, send_sem=gather_out.at[way, n], recv_sem=gather_in.at[way, n],
            device_id=(dom, gather_to[way]), device_id_type=MESH,
        )

    sent = []

    def send(way, n, owner, part):
        copy = piece(way, n, owner, part)
        copy.start()
        sent.append(copy)

    def received(way, n, owner, part):
        piece(way, n, owner, part).wait_recv()

    fetches[0].wait()
    for part in range(PARTS):
        for p in range(part * PROJ_PART, (part + 1) * PROJ_PART):
            for g in range(4):
                x = proj_ref[pl.ds(64 * g + p, 8, stride=8), :]
                pbuf[band, p, :, pl.ds(128 * g, 128)] = transposed_parts(x)
        if part == 0:
            pl.semaphore_wait(barrier, 3 + 2 * sum(inside(step).astype(jnp.int32) for step in REACHED))
        for way in (2, 0, 1):
            send(way, part, band, part)

    def halo_copy(app, side, source):
        planes = pl.ds(CX - REACH, REACH) if side == 0 else pl.ds(0, REACH)
        return pltpu.make_async_remote_copy(
            src_ref=source.at[planes], dst_ref=halo.at[app, side],
            send_sem=halo_out.at[app, side], recv_sem=halo_in_sem.at[app, side],
            device_id=(dom + (1 if side == 0 else -1), band), device_id_type=MESH,
        )

    def part_copy(app, n):
        return pltpu.make_async_remote_copy(
            src_ref=part_own.at[app], dst_ref=part_in.at[app, n],
            send_sem=part_out_sem.at[app, n], recv_sem=part_in_sem.at[app, n],
            device_id=(dom + REACHED[n], band), device_id_type=MESH,
        )

    def mate_copy():
        return pltpu.make_async_remote_copy(
            src_ref=wave_ref.at[pl.ds((SX // 2) * (1 - z), SX)], dst_ref=mate_field,
            send_sem=mate_out_sem.at[0], recv_sem=mate_in_sem.at[0],
            device_id=(dom, gather_to[2]), device_id_type=MESH,
        )

    def mate_part_copy(n):
        return pltpu.make_async_remote_copy(
            src_ref=mate_part, dst_ref=mate_part_in.at[n],
            send_sem=mate_out_sem.at[1 + n], recv_sem=mate_in_sem.at[1 + n],
            device_id=(dom + REACHED_BY_MATE[n], gather_to[2]), device_id_type=MESH,
        )

    def kb_copy(n):
        return pltpu.make_async_remote_copy(
            src_ref=kb_own, dst_ref=kb_in.at[n], send_sem=kb_out_sem.at[n], recv_sem=kb_in_sem.at[n],
            device_id=(dom + (1 if n == 0 else -1), band), device_id_type=MESH,
        )

    def field(app):
        return wave_ref if app == 0 else fields.at[app - 1]

    for fetch in fetches[1:]:
        fetch.wait()
    kb_own[:, 0:ATOM_DEV] = kb_fetched[...]
    mate_copy().start()
    for n in range(2):
        where_inside(SIDES[n], kb_copy(n).start)
    for side in range(2):
        where_inside(SIDES[side], halo_copy(0, side, field(0)).start)

    def make_picks():
        lane = iota((8, 128), 1)
        lane_slot, lane_cell = lane >> 4, lane & 15
        pad_rows = iota((128, 128), 0)
        first_atom = (dom - 1) * ATOM_DEV
        for g in range(4):
            at_x, at_z, atom = (jnp.zeros((8, 128), jnp.int32) for _ in range(3))
            for q in range(8):
                here = lane_slot == q
                at_x = jnp.where(here, corner_ref[0, 8 * g + q], at_x)
                at_z = jnp.where(here, corner_ref[2, 8 * g + q], at_z)
                atom = jnp.where(here, atom_ref[8 * g + q] - first_atom, atom)
            lanes = pl.ds(128 * g, 128)
            x_corner[:, lanes] = at_x
            hot_z = jnp.where(pad_rows == (at_z + lane_cell)[0:1, :], F32(1.0), F32(0.0))
            pick_z[0:CZ, lanes] = pick_z[CZ:, lanes] = hot_z.astype(BF16)
            pick_zt[lanes, :] = jnp.transpose(hot_z).astype(BF16)
            hot_atom = jnp.where(pad_rows == atom[0:1, :], F32(1.0), F32(0.0))
            pick_atom[:, lanes] = hot_atom.astype(BF16)
            pick_atom_t[lanes, :] = jnp.transpose(hot_atom).astype(BF16)

    def extract(planes, out):
        count = out.shape[0] // 2
        extent = count + CX - SX
        rows = halves_beside(planes[...].reshape(extent * CY, CZ))
        for g in range(4):
            lanes = pl.ds(128 * g, 128)
            along_z = dot(rows, pick_z[:, lanes]).reshape(extent, CY, 128)
            at_x = x_corner[:, lanes][None, 0:1, :]
            cut = along_z[0:count]
            for d in range(1, CX - SX + 1):
                cut = jnp.where(at_x == d, along_z[d : d + count], cut)
            out[:, :, lanes] = cut.reshape(2 * count, 8, 128)

    def make_stencil():
        distance = jnp.abs(iota((CZ, CZ), 0) - iota((CZ, CZ), 1))
        band_z[:, 0:128], band_z[:, 128:256] = split(weight_at(distance, 3.0 * KINETIC[0]))
        row, col = iota((ROWS, ROWS), 0), iota((ROWS, ROWS), 1)
        gap_x, gap_y = jnp.abs((row >> 4) - (col >> 4)), jnp.abs((row & 15) - (col & 15))
        gap = jnp.where(gap_x == 0, gap_y, jnp.where(gap_y == 0, gap_x, 99))
        cross[0:ROWS, :], cross[ROWS:, :] = split(weight_at(gap, 0.0))

    def accumulate(step, part, own=True, mate=True):
        owner, at = band_at(step, False), lax.rem(y + step + Y_RING, Y_RING)
        here = pl.ds(part * PROJ_PART, PROJ_PART)
        values = pbuf[owner, here]
        for wanted, total, cells in ((own, acc, boxes[owner]), (mate, mate_acc, mate_boxes[at])):
            if wanted:
                term = values * cells[None]
                total[here] = term if step == 0 else total[here] + term

    def atom_partials(total):
        by_slot = jnp.sum(total[...], axis=1)
        return dot_below(by_slot, pick_atom_t[...])

    def apply_local(app):
        rows = field(app)[...].reshape(ROWS, CZ)
        high, low = split(rows)
        weights = band_z[...]
        both = dot(high, weights)
        out = both[:, 0:128] + both[:, 128:256] + dot(low, weights[:, 0:128])
        both = dot(cross[...], jnp.concatenate([high, low], axis=1))
        out = out + (both[0:ROWS, 0:128] + both[0:ROWS, 128:256] + both[ROWS:, 0:128])
        out = out + pot_ref[...].reshape(ROWS, CZ) * rows
        local[...] = out.reshape(CX, CY, CZ)

    def add_halo(app):
        for side in range(2):
            where_inside(-SIDES[side], halo_copy(app, side, field(app)).wait_recv)
        low = jnp.where(dom > 0, halo[app, 0], F32(0.0))
        high = jnp.where(dom < doms - 1, halo[app, 1], F32(0.0))
        for x in range(REACH):
            local[x] = local[x] + sum(F32(KINETIC[k]) * low[REACH + x - k] for k in range(x + 1, REACH + 1))
            at = CX - 1 - x
            local[at] = local[at] + sum(F32(KINETIC[k]) * high[k - 1 - x] for k in range(x + 1, REACH + 1))

    all_parts = tuple(range(PARTS))
    halves = all_parts[:HALF], all_parts[HALF:]
    ways = ((0, -1), (1, 1))
    z_expected = [(band_at(0, True), part) for part in all_parts]
    z_waiting = []

    def to_mate(step, part):
        z_waiting.append((step, part))

    def flush_to_mate():
        for step, part in z_waiting:
            send(2, len(z_expected), band_at(step, False), part)
            z_expected.append((band_at(step, True), part))
        z_waiting.clear()

    def other_ring(hop, part):
        return 3 * PARTS + HALF + sum(RING_PARTS[: hop + 1]) + part - PARTS

    def pass_other(hop):
        for part in range(PARTS - RING_PARTS[max(hop - 1, 0)], PARTS):
            for way, sign in ways:
                owner = band_at(sign * hop, True)
                if hop:
                    received(way, other_ring(hop - 1, part), owner, part)
                elif way == 0:
                    received(2, part, owner, part)
                if hop < 3 and part >= PARTS - RING_PARTS[hop]:
                    send(way, other_ring(hop, part), owner, part)

    for step in range(1, 4):
        for part in all_parts:
            for way, sign in ways:
                owner = band_at(sign * step, False)
                received(way, (step - 1) * PARTS + part, owner, part)
                if step < 3:
                    send(way, step * PARTS + part, owner, part)
                elif part in halves[way]:
                    send(way, 3 * PARTS + part - halves[way][0], owner, part)
                if part < PARTS - RING_PARTS[step - 1]:
                    to_mate(sign * step, part)
                    flush_to_mate()
        pass_other(step - 1)
        if step == 1:
            make_picks()
            extract(field(0), boxes)
            for part in all_parts:
                accumulate(0, part, mate=False)
                for sign in (-1, 1):
                    accumulate(sign, part, mate=False)
        elif step == 2:
            mate_copy().wait_recv()
            extract(mate_field, mate_boxes)
            for part in all_parts:
                accumulate(0, part, own=False)
                for sign in (-1, 1):
                    accumulate(sign, part, own=False)
                    accumulate(2 * sign, part)
        else:
            for part in all_parts:
                for sign in (-1, 1):
                    accumulate(3 * sign, part)
    for part in range(HALF):
        for way, sign in ways:
            at = halves[way][part]
            received(way, 3 * PARTS + part, band_at(4, False), at)
            to_mate(4, at)
            flush_to_mate()
            accumulate(4, at)
    mate_part[...] = atom_partials(mate_acc)
    for n in range(len(REACHED)):
        where_inside(REACHED[n], mate_part_copy(n + 1).start)
    mate_part_copy(0).start()
    part_own[0] = atom_partials(acc)
    for n in range(len(REACHED)):
        where_inside(REACHED[n], part_copy(0, n).start)
    pass_other(3)
    make_stencil()
    apply_local(0)
    for n, (owner, part) in enumerate(z_expected):
        if n >= PARTS or part < PARTS - RING_PARTS[0]:
            received(2, n, owner, part)
    add_halo(0)

    for n in range(2):
        where_inside(-SIDES[n], kb_copy(n).wait_recv)
    atom_lane = iota((8, 128), 1)
    energy = jnp.where(
        atom_lane < ATOM_DEV,
        jnp.where(dom > 0, kb_in[0], F32(0.0)),
        jnp.where(
            atom_lane < 2 * ATOM_DEV,
            pltpu.roll(kb_own[...], ATOM_DEV, 1),
            jnp.where((atom_lane < 3 * ATOM_DEV) & (dom < doms - 1), pltpu.roll(kb_in[1], 2 * ATOM_DEV, 1), F32(0.0)),
        ),
    )
    def all_left(app):
        if app == 0:
            for copy in sent:
                copy.wait_send()
            mate_copy().wait_send()
            for n in range(len(REACHED_BY_MATE)):
                where_inside(REACHED_BY_MATE[n], mate_part_copy(n).wait_send)
            for n in range(2):
                where_inside(SIDES[n], kb_copy(n).wait_send)
        for side in range(2):
            where_inside(SIDES[side], halo_copy(app, side, field(app)).wait_send)
        for n in range(len(REACHED)):
            where_inside(REACHED[n], part_copy(app, n).wait_send)

    centre, coefs = coefficients()
    for app in range(DEGREE):
        if app:
            extract(field(app), boxes)
            for g in range(4):
                lanes = pl.ds(128 * g, 128)
                total = pbuf[0, :, :, lanes] * boxes[0, :, lanes][None]
                for owner in range(1, 2 * SX):
                    total = total + pbuf[owner, :, :, lanes] * boxes[owner, :, lanes][None]
                acc[:, :, lanes] = total
            part_own[app] = atom_partials(acc)
            for n in range(len(REACHED)):
                where_inside(REACHED[n], part_copy(app, n).start)
            for side in range(2):
                where_inside(SIDES[side], halo_copy(app, side, field(app)).start)
            apply_local(app)
            all_left(app - 1)
            add_halo(app)
        total = part_own[app]
        if app == 0:
            mate_part_copy(0).wait_recv()
            total = total + mate_part_in[0]
        for n, step in enumerate(REACHED):
            where_inside(-step, part_copy(app, n).wait_recv)
            partial = part_in[app, n]
            if app == 0:
                where_inside(-step, mate_part_copy(n + 1).wait_recv)
                partial = partial + mate_part_in[n + 1]
            shifted = pltpu.roll(partial, (-step * ATOM_DEV) % 128, 1)
            total = total + jnp.where(inside(-step), shifted, F32(0.0))
        back_all = dot_below(total * energy, pick_atom[...])
        for g in range(4):
            lanes = pl.ds(128 * g, 128)
            back = back_all[:, 128 * g : 128 * (g + 1)]
            weights = [jnp.broadcast_to(back[p : p + 1, :], (8, 128)) for p in range(PROJ)]
            at_x = x_corner[:, lanes]
            for half in range(2):
                values = []
                for i in range(SX):
                    value = pbuf[2 * i + half, 0, :, lanes] * weights[0]
                    for p in range(1, PROJ):
                        value = value + pbuf[2 * i + half, p, :, lanes] * weights[p]
                    values.append(value)
                for x in range(CX):
                    spread = jnp.zeros((8, 128), F32)
                    for d in range(max(0, x - SX + 1), min(x, CX - SX) + 1):
                        spread = jnp.where(at_x == d, values[x - d], spread)
                    deposit_in[pl.ds(x * CY + 8 * half, 8), lanes] = spread
        nonlocal_part = dot_below(deposit_in[...], pick_zt[...]).reshape(CX, CY, CZ)
        now = field(app)[...]
        scale, keep = coefs[app]
        new = F32(scale) * (local[...] + nonlocal_part - F32(centre) * now)
        if app:
            new = new - F32(keep) * field(app - 1)[...]
        if app < DEGREE - 1:
            fields[app] = new
        else:
            out_ref[0] = new

    all_left(DEGREE - 1)


def on_device(wave_block, potential, projectors, kb_energy, slot_atom, slot_corner):
    vmem, hbm = pl.BlockSpec(memory_space=pltpu.VMEM), pl.BlockSpec(memory_space=pltpu.HBM)
    dma = pltpu.SemaphoreType.DMA
    return pl.pallas_call(
        kernel,
        out_shape=jax.ShapeDtypeStruct(wave_block.shape, F32),
        in_specs=[hbm] * 6,
        out_specs=vmem,
        scratch_shapes=[
            pltpu.VMEM((CX, CY, CZ), F32),
            pltpu.VMEM((CX, CY, CZ), F32),
            pltpu.VMEM((SLOTS * PROJ + 8, 128), F32),
            pltpu.VMEM((8, ATOM_DEV), F32),
            pltpu.SMEM((SLOTS,), jnp.int32),
            pltpu.SMEM((3, SLOTS), jnp.int32),
            dma((6,)),
            pltpu.VMEM((2 * SX, PROJ, 8, LANES), F32),
            pltpu.VMEM((DEGREE, 2, REACH, CY, CZ), F32),
            pltpu.VMEM((DEGREE, 8, 128), F32),
            pltpu.VMEM((DEGREE, len(REACHED), 8, 128), F32),
            pltpu.VMEM((8, 128), F32),
            pltpu.VMEM((2, 8, 128), F32),
            pltpu.VMEM((DEGREE - 1, CX, CY, CZ), F32),
            pltpu.VMEM((2 * SX, 8, LANES), F32),
            pltpu.VMEM((PROJ, 8, LANES), F32),
            pltpu.VMEM((ROWS, LANES), F32),
            pltpu.VMEM((SX, CY, CZ), F32),
            pltpu.VMEM((SX, 8, LANES), F32),
            pltpu.VMEM((PROJ, 8, LANES), F32),
            pltpu.VMEM((8, 128), F32),
            pltpu.VMEM((len(REACHED_BY_MATE), 8, 128), F32),
            pltpu.VMEM((2 * CZ, LANES), BF16),
            pltpu.VMEM((LANES, CZ), BF16),
            pltpu.VMEM((128, LANES), BF16),
            pltpu.VMEM((LANES, 128), BF16),
            pltpu.VMEM((CZ, 256), BF16),
            pltpu.VMEM((2 * ROWS, ROWS), BF16),
            pltpu.VMEM((8, LANES), jnp.int32),
            pltpu.VMEM((CX, CY, CZ), F32),
            dma((3, SENDS)),
            dma((3, SENDS)),
            dma((1 + len(REACHED_BY_MATE),)),
            dma((1 + len(REACHED_BY_MATE),)),
            dma((DEGREE, 2)),
            dma((DEGREE, 2)),
            dma((DEGREE, len(REACHED))),
            dma((DEGREE, len(REACHED))),
            dma((2,)),
            dma((2,)),
        ],
        compiler_params=pltpu.CompilerParams(
            collective_id=0, has_side_effects=True, vmem_limit_bytes=56 * 1024 * 1024
        ),
        name="chebyshev",
    )(wave_block, potential, projectors.reshape(SLOTS * PROJ, 128), kb_energy.T, slot_atom, slot_corner)


def solution(mesh):
    placed = (
        P("band", "dom", None, None),
        P("dom", None, None),
        P("dom", None, "band"),
        P("dom", None),
        P("dom"),
        P(None, "dom"),
    )
    return jax.shard_map(
        on_device,
        mesh=mesh,
        in_specs=placed,
        out_specs=P("band", "dom", None, None),
        check_vma=False,
    )
```
